32 devices in a mesh: cell: 8 (over y, x, core), blk: 4 (over z).
Axes of the slice: x: 2, y: 2, z: 4, core: 2. Of those that a mesh axis runs over, the one named last changes fastest.
Arguments:
- snapshots: float32 [128, 16384], P('blk', 'cell'), may hold values from -100 to 100
- plan: int32 [31, 32], replicated, may hold values from 0 to 31, as said below
Outputs:
- energy_field: float32 [128, 16384], P('blk', 'cell')
- mode_energy: float32 [128], P('blk')
The draws below stay inside these ranges and needn't reach their ends.
Inputs may be any that keep to these rules, and one draw needn't show every extreme that they name: `plan`: each row pairs every index 0 .. 31 with exactly one other index (the partner's partner is the index itself, never the index), and over all rows every two indices are paired exactly once.
All inputs are finite; a program needn't handle non-finite values.
Results may differ from the reference program's by a relative error of at most 0.0055.
Values sent between devices are 32-bit elements; how exact they have to be, the bound alone decides.
No kernel may reach another device: no remote copies, remote signals or barrier semaphores. Data moves between devices by JAX's collectives and lax.ppermute only.
A program may use at most 64 MiB of HBM per device.

```python
from functools import partial
import jax
import jax.numpy as jnp
from jax import lax

BW = 16
PAIRW = 32
COLS = 128
ROWS = 16384
ROUNDS = 7
N_BLK = 4


def draw_snapshots(key, part):
    key_column, key_row, key_noise = jax.random.split(jax.random.fold_in(key, 11), 3)
    column_scale = jnp.exp(jax.random.uniform(key_column, (COLS, 1), jnp.float32, jnp.log(0.3), jnp.log(3.0)))
    row_scale = jnp.exp(jax.random.uniform(key_row, (1, ROWS), jnp.float32, jnp.log(0.3), jnp.log(3.0)))
    values = jnp.clip(jax.random.normal(key_noise, (COLS, ROWS), jnp.float32), -5.0, 5.0)
    return (values * column_scale * row_scale).astype(jnp.float32)


def draw_plan(key, part):
    players = PAIRW - 1
    relabel = jax.random.permutation(jax.random.fold_in(key, 23), PAIRW).astype(jnp.int32)
    steps_col = jnp.arange(players, dtype=jnp.int32)[:, None]
    indices = jnp.arange(PAIRW, dtype=jnp.int32)[None, :]
    mirrored = jnp.mod(2 * steps_col - indices, players)
    circle_table = jnp.where(indices == players, steps_col, jnp.where(mirrored == indices, players, mirrored))
    circle_table = circle_table.astype(jnp.int32)
    mapped = relabel[circle_table]
    table = jnp.zeros((players, PAIRW), jnp.int32).at[:, relabel].set(mapped)
    return table


def setup_inputs(seed: int = 0) -> dict:
    seeds = jax.random.split(jax.random.key(seed), 3)
    snapshots = draw_snapshots(jax.random.fold_in(seeds[2], 71), 0)
    plan = draw_plan(jax.random.fold_in(seeds[2], 71), 0)
    return dict(snapshots=snapshots, plan=plan)


def inner_sweep(gram_whole, plan):
    pair_width = gram_whole.shape[0]
    positions = jnp.arange(pair_width, dtype=jnp.int32)

    def one_step(step_index, loop_state):
        gram_now, accumulated = loop_state
        partner = lax.dynamic_index_in_dim(plan, step_index, 0, keepdims=False)
        onehot = (partner[:, None] == positions[None, :]).astype(jnp.float32)
        symmetric = 0.5 * (gram_now + gram_now.T)
        own_diag = jnp.diagonal(symmetric)
        cross_term = jnp.sum(onehot * symmetric, axis=1)
        other_diag = jnp.sum(onehot * own_diag[None, :], axis=1)
        is_lower = positions < partner
        spread = jnp.where(is_lower, own_diag - other_diag, other_diag - own_diag)
        angles = 0.5 * jnp.arctan2(2.0 * cross_term, spread)
        cosine = jnp.cos(angles)
        sine_part = jnp.where(is_lower, jnp.sin(angles), -jnp.sin(angles))
        rotation_step = jnp.diag(cosine) + (onehot * sine_part[:, None]).T
        gram_now = jnp.dot(jnp.dot(rotation_step.T, gram_now, precision=lax.Precision.HIGHEST), rotation_step, precision=lax.Precision.HIGHEST)
        accumulated = jnp.dot(accumulated, rotation_step, precision=lax.Precision.HIGHEST)
        return gram_now, accumulated

    initial = (gram_whole, jnp.eye(pair_width, dtype=jnp.float32))
    return lax.fori_loop(0, pair_width - 1, one_step, initial)[1]


def pair_turn(stacked_pair, plan):
    gram_whole = jnp.dot(stacked_pair, stacked_pair.T, precision=lax.Precision.HIGHEST)
    turning = inner_sweep(gram_whole, plan)
    return jnp.dot(turning.T, stacked_pair, precision=lax.Precision.HIGHEST)


def reference(snapshots, plan):
    arranged = snapshots.reshape(N_BLK, 2, BW, ROWS)

    def one_round(loop_state, unused):
        upper_blocks, lower_blocks = loop_state
        stacked = jnp.concatenate([upper_blocks, lower_blocks], axis=1)
        turned = lax.map(partial(pair_turn, plan=plan), stacked)
        upper_new = turned[:, :BW]
        lower_new = turned[:, BW:]
        new_upper = jnp.concatenate([upper_new[:1], lower_new[:1], upper_new[1:-1]], axis=0)
        new_lower = jnp.concatenate([lower_new[1:], upper_new[-1:]], axis=0)
        return (new_upper, new_lower), None

    final_state, unused = lax.scan(one_round, (arranged[:, 0], arranged[:, 1]), None, length=ROUNDS)
    finished = jnp.concatenate([final_state[0], final_state[1]], axis=1).reshape(COLS, ROWS)
    energy_field = finished * finished
    mode_energy = jnp.sum(energy_field, axis=1) / ROWS
    return energy_field, mode_energy
```

```python
import functools

import jax
import jax.numpy as jnp
from jax import lax
from jax.experimental import pallas as pl
from jax.experimental.pallas import tpu as pltpu
from jax.sharding import PartitionSpec as P

ROUNDS = 7
TINY_SQUARE = 2.0**-78
UP = 2.0**80
FLOOR = 2.0**-124
FLOOR_ROOT = 2.0**-62
LANES = 128


def split3(x):
    high = x.astype(jnp.bfloat16)
    rest = x - high.astype(jnp.float32)
    middle = rest.astype(jnp.bfloat16)
    low = (rest - middle.astype(jnp.float32)).astype(jnp.bfloat16)
    return high, middle, low


def dot_full(a, b, contract_a=1, contract_b=0):
    a0, a1, a2 = split3(a)
    b0, b1, b2 = split3(b)

    def one(x, y):
        return lax.dot_general(
            x, y, (((contract_a,), (contract_b,)), ((), ())), preferred_element_type=jnp.float32
        )

    small = one(a0, b2) + one(a2, b0) + one(a1, b1)
    return one(a0, b0) + ((one(a0, b1) + one(a1, b0)) + small)


def half_angle(twice_cross, spread, sign):
    up_cross, up_spread = twice_cross * UP, spread * UP
    square = spread * spread + twice_cross * twice_cross
    up_square = up_spread * up_spread + up_cross * up_cross
    is_small = square < TINY_SQUARE
    norm_square = jnp.maximum(jnp.where(is_small, up_square, square), FLOOR)
    size = jnp.maximum(jnp.abs(jnp.where(is_small, up_spread, spread)), FLOOR_ROOT)
    half_cross = jnp.where(is_small, up_cross, twice_cross) * (0.5 * sign)
    cross_sign = jnp.where(twice_cross < 0, -sign, sign)
    inverse = lax.rsqrt(norm_square)
    large_square = 0.5 * (size * inverse) + 0.5
    root = lax.rsqrt(large_square)
    large = large_square * root
    small = (half_cross * inverse) * root
    in_order = spread >= 0
    cosine = jnp.where(in_order, large, jnp.abs(small))
    sine = jnp.where(in_order, small, cross_sign * large)
    return cosine, sine


def gather(x, index):
    return jnp.take_along_axis(x, jnp.broadcast_to(index, x.shape), axis=1)


def tall(x, like):
    return jnp.concatenate([x] * (like.shape[0] // x.shape[0]), axis=0)


def turned_by(c, s, x, y):
    return tall(c, x) * x + tall(s, x) * y


def both(wx, tx, wy, ty):
    return jnp.sum(wx * ty + wy * tx, axis=0, keepdims=True)


def new_diagonal(cosine, sine, twice_cross, own, other):
    return (cosine * cosine) * own + (cosine * sine) * twice_cross + (sine * sine) * other


def single_step(state, index, signs):
    w, t, d = state
    p = index[0:1]
    wp, tp, dp = gather(w, p), gather(t, p), gather(d, p)
    sign = signs[0:1]
    cross = both(w, t, wp, tp)
    c, s = half_angle(cross, (d - dp) * sign, sign)
    return turned_by(c, s, w, wp), turned_by(c, s, t, tp), new_diagonal(c, s, cross, d, dp)


def double_step(state, index, signs):
    w, t, d = state
    p, q, pq = index[0:1], index[1:2], index[2:3]
    sign, sign_q, sign_next = signs[0:1], signs[1:2], signs[2:3]
    wp, tp, dp = gather(w, p), gather(t, p), gather(d, p)
    wq, tq, dq = gather(w, q), gather(t, q), gather(d, q)
    wpq, tpq, dpq = gather(w, pq), gather(t, pq), gather(d, pq)
    cross = both(w, t, wp, tp)
    cross_q = both(wq, tq, wpq, tpq)
    e00, e01 = both(w, t, wq, tq), both(w, t, wpq, tpq)
    e10, e11 = both(wp, tp, wq, tq), both(wp, tp, wpq, tpq)
    c, s = half_angle(cross, (d - dp) * sign, sign)
    cq, sq = half_angle(cross_q, (dq - dpq) * sign_q, sign_q)
    cross_next = ((c * cq) * e00 + (s * sq) * e11) + ((c * sq) * e01 + (s * cq) * e10)
    d1 = new_diagonal(c, s, cross, d, dp)
    d1q = new_diagonal(cq, sq, cross_q, dq, dpq)
    c1, s1 = half_angle(cross_next, (d1 - d1q) * sign_next, sign_next)
    w1, t1 = turned_by(c, s, w, wp), turned_by(c, s, t, tp)
    w1q, t1q = turned_by(cq, sq, wq, wpq), turned_by(cq, sq, tq, tpq)
    return (
        turned_by(c1, s1, w1, w1q),
        turned_by(c1, s1, t1, t1q),
        new_diagonal(c1, s1, cross_next, d1, d1q),
    )


def turn_kernel(n_steps, gram_ref, index_ref, sign_ref, modes_ref, energy_ref, c_ref):
    cols = gram_ref.shape[0]
    pair = 32
    half = pair // 2
    tiles = cols // LANES
    lane = lax.broadcasted_iota(jnp.int32, (pair, cols), 1)
    row = lax.broadcasted_iota(jnp.int32, (pair, cols), 0)
    is_diag = row == lane % pair
    start = is_diag.astype(jnp.float32)
    own_pair = lax.broadcasted_iota(jnp.int32, (cols, cols), 0) // pair == (
        lax.broadcasted_iota(jnp.int32, (cols, cols), 1) // pair
    )
    c_ref[...] = gram_ref[...]
    modes_ref[...] = (
        lax.broadcasted_iota(jnp.int32, (cols, cols), 0) == lax.broadcasted_iota(jnp.int32, (cols, cols), 1)
    ).astype(jnp.float32)

    def moved(x):
        place = lax.broadcasted_iota(jnp.int32, x.shape, 1)
        is_upper = place % pair < half
        from_own = (place < half) & is_upper
        shifted = ((place // pair == 1) & is_upper) | (place >= cols - half)
        right, left, by_half = pltpu.roll(x, pair, 1), pltpu.roll(x, cols - pair, 1), pltpu.roll(x, half, 1)
        return jnp.where(from_own, x, jnp.where(shifted, by_half, jnp.where(is_upper, right, left)))

    def one_round(round_index, carry):
        kept = jnp.where(own_pair, c_ref[...], 0.0)
        w = kept[0:pair]
        for p in range(1, cols // pair):
            w = w + kept[p * pair : (p + 1) * pair]
        d = jnp.broadcast_to(jnp.sum(jnp.where(is_diag, w, 0.0), axis=0, keepdims=True), (8, cols))
        turned, energies = [], []
        for tile in range(tiles):
            at = slice(tile * LANES, (tile + 1) * LANES)
            state = (w[:, at], start[:, at], d[:, at])

            def steps(k, state):
                return double_step(state, index_ref[k], sign_ref[k])

            state = lax.fori_loop(0, n_steps // 2, steps, state)
            if n_steps % 2:
                state = single_step(state, index_ref[n_steps // 2], sign_ref[n_steps // 2])
            turned.append(state[1])
            energies.append(state[2])
        t = moved(jnp.concatenate(turned, axis=1) if tiles > 1 else turned[0])
        d = jnp.concatenate(energies, axis=1) if tiles > 1 else energies[0]
        energy_ref[...] = moved(d)
        lanes_from = moved(lax.broadcasted_iota(jnp.int32, (8, cols), 1))[0:1] // pair
        rows_pair = lax.broadcasted_iota(jnp.int32, (cols, cols), 0) // pair
        whole = jnp.where(rows_pair == lanes_from, jnp.concatenate([t] * (cols // pair), axis=0), 0.0)
        half_way = dot_full(c_ref[...], whole)
        c_ref[...] = dot_full(whole, half_way, 0, 0)
        modes_ref[...] = dot_full(modes_ref[...], whole)
        return carry

    lax.fori_loop(0, ROUNDS, one_round, 0)


def turn_all(gram, plan):
    cols = gram.shape[0]
    n_steps, pair = plan.shape
    pairs = (n_steps + 1) // 2
    here = jnp.arange(pair, dtype=jnp.int32)
    first = plan[0::2]
    second = jnp.concatenate([plan[1::2], here[None]], axis=0)[:pairs]
    first_of_second = jnp.take_along_axis(first, second, axis=1)
    index = jnp.stack([first, second, first_of_second], axis=1)
    index = jnp.concatenate([index + 32 * g for g in range(LANES // 32)], axis=2)

    def sign_of(own, other):
        return jnp.where(own < other, 1.0, -1.0).astype(jnp.float32)

    signs = jnp.stack(
        [sign_of(here[None], first), sign_of(second, first_of_second), sign_of(here[None], second)], axis=1
    )
    signs = jnp.concatenate([signs] * (LANES // 32), axis=2)
    return pl.pallas_call(
        functools.partial(turn_kernel, n_steps),
        out_shape=(
            jax.ShapeDtypeStruct((cols, cols), jnp.float32),
            jax.ShapeDtypeStruct((8, cols), jnp.float32),
        ),
        in_specs=[pl.BlockSpec(memory_space=pltpu.VMEM)] * 3,
        out_specs=[pl.BlockSpec(memory_space=pltpu.VMEM)] * 2,
        scratch_shapes=[pltpu.VMEM((cols, cols), jnp.float32)],
        compiler_params=pltpu.CompilerParams(vmem_limit_bytes=48 * 1024 * 1024),
    )(gram, index, signs)


def summed_over_all(x):
    n = lax.axis_size("cell") * lax.axis_size("blk")
    rows, cols = x.shape
    pieces = lax.all_to_all(x.reshape(n, rows // n, cols), ("cell", "blk"), 0, 0)
    total = jnp.sum(pieces, axis=0)
    return lax.all_to_all(
        jnp.broadcast_to(total[None], (n,) + total.shape), ("cell", "blk"), 0, 0
    ).reshape(rows, cols)


def on_device(snapshots, plan):
    pair, cells = snapshots.shape
    n_blk = lax.axis_size("blk")
    cols = pair * n_blk
    part = lax.all_to_all(snapshots.reshape(pair, n_blk, cells // n_blk), "blk", 1, 0)
    part = part.reshape(cols, cells // n_blk)
    gathered = lax.all_gather(snapshots, "blk", axis=0, tiled=True)
    gram = summed_over_all(
        lax.dot_general(part, part, (((1,), (1,)), ((), ())), precision=lax.Precision.HIGHEST)
    )
    modes, energy = turn_all(gram, plan)
    place = lax.axis_index("blk") * pair
    own = lax.dynamic_slice_in_dim(modes, place, pair, 1)
    rotated = lax.dot_general(own, gathered, (((0,), (0,)), ((), ())), precision=lax.Precision.HIGHEST)
    mode_energy = lax.dynamic_slice_in_dim(energy[0], place, pair, 0) / (cells * lax.axis_size("cell"))
    return rotated * rotated, mode_energy


def solution(mesh):
    return jax.shard_map(
        on_device,
        mesh=mesh,
        in_specs=(P("blk", "cell"), P()),
        out_specs=(P("blk", "cell"), P("blk")),
        check_vma=False,
    )
```

```python
import functools

import jax
import jax.numpy as jnp
from jax import lax
from jax.experimental import pallas as pl
from jax.experimental.pallas import tpu as pltpu
from jax.sharding import PartitionSpec as P

ROUNDS = 7
TINY_SQUARE = 2.0**-78
UP = 2.0**80
FLOOR = 2.0**-124
FLOOR_ROOT = 2.0**-62
LANES = 128


def split3(x):
    high = x.astype(jnp.bfloat16)
    rest = x - high.astype(jnp.float32)
    middle = rest.astype(jnp.bfloat16)
    low = (rest - middle.astype(jnp.float32)).astype(jnp.bfloat16)
    return high, middle, low


def dot_full(a, b, contract_a=1, contract_b=0):
    a0, a1, a2 = split3(a)
    b0, b1, b2 = split3(b)

    def one(x, y):
        return lax.dot_general(
            x, y, (((contract_a,), (contract_b,)), ((), ())), preferred_element_type=jnp.float32
        )

    small = one(a0, b2) + one(a2, b0) + one(a1, b1)
    return one(a0, b0) + ((one(a0, b1) + one(a1, b0)) + small)


def half_angle(twice_cross, spread, sign):
    up_cross, up_spread = twice_cross * UP, spread * UP
    square = spread * spread + twice_cross * twice_cross
    up_square = up_spread * up_spread + up_cross * up_cross
    is_small = square < TINY_SQUARE
    norm_square = jnp.maximum(jnp.where(is_small, up_square, square), FLOOR)
    size = jnp.maximum(jnp.abs(jnp.where(is_small, up_spread, spread)), FLOOR_ROOT)
    half_cross = jnp.where(is_small, up_cross, twice_cross) * (0.5 * sign)
    cross_sign = jnp.where(twice_cross < 0, -sign, sign)
    inverse = lax.rsqrt(norm_square)
    large_square = 0.5 * (size * inverse) + 0.5
    root = lax.rsqrt(large_square)
    large = large_square * root
    small = (half_cross * inverse) * root
    in_order = spread >= 0
    cosine = jnp.where(in_order, large, jnp.abs(small))
    sine = jnp.where(in_order, small, cross_sign * large)
    return cosine, sine


def gather(x, index):
    return jnp.take_along_axis(x, jnp.broadcast_to(index, x.shape), axis=1)


def tall(x, like):
    return jnp.concatenate([x] * (like.shape[0] // x.shape[0]), axis=0)


def turned_by(c, s, x, y):
    return tall(c, x) * x + tall(s, x) * y


def both(wx, tx, wy, ty):
    return jnp.sum(wx * ty + wy * tx, axis=0, keepdims=True)


def new_diagonal(cosine, sine, twice_cross, own, other):
    return (cosine * cosine) * own + (cosine * sine) * twice_cross + (sine * sine) * other


def single_step(state, index, signs):
    w, t, d = state
    (p,) = index
    wp, tp, dp = gather(w, p), gather(t, p), gather(d, p)
    (sign,) = signs
    cross = both(w, t, wp, tp)
    c, s = half_angle(cross, (d - dp) * sign, sign)
    return turned_by(c, s, w, wp), turned_by(c, s, t, tp), new_diagonal(c, s, cross, d, dp)


def double_step(state, index, signs):
    w, t, d = state
    p, q, pq = index
    sign, sign_q, sign_next = signs
    wp, tp, dp = gather(w, p), gather(t, p), gather(d, p)
    wq, tq, dq = gather(w, q), gather(t, q), gather(d, q)
    wpq, tpq, dpq = gather(w, pq), gather(t, pq), gather(d, pq)
    cross = both(w, t, wp, tp)
    cross_q = both(wq, tq, wpq, tpq)
    e00, e01 = both(w, t, wq, tq), both(w, t, wpq, tpq)
    e10, e11 = both(wp, tp, wq, tq), both(wp, tp, wpq, tpq)
    c, s = half_angle(cross, (d - dp) * sign, sign)
    cq, sq = half_angle(cross_q, (dq - dpq) * sign_q, sign_q)
    cross_next = ((c * cq) * e00 + (s * sq) * e11) + ((c * sq) * e01 + (s * cq) * e10)
    d1 = new_diagonal(c, s, cross, d, dp)
    d1q = new_diagonal(cq, sq, cross_q, dq, dpq)
    c1, s1 = half_angle(cross_next, (d1 - d1q) * sign_next, sign_next)
    w1, t1 = turned_by(c, s, w, wp), turned_by(c, s, t, tp)
    w1q, t1q = turned_by(cq, sq, wq, wpq), turned_by(cq, sq, tq, tpq)
    return (
        turned_by(c1, s1, w1, w1q),
        turned_by(c1, s1, t1, t1q),
        new_diagonal(c1, s1, cross_next, d1, d1q),
    )


def turn_kernel(n_steps, gram_ref, plan_ref, place_ref, modes_ref, energy_ref, c_ref, q_ref, index_ref, sign_ref):
    cols = gram_ref.shape[0]
    pair = plan_ref.shape[1]
    half = pair // 2
    tiles = cols // LANES
    lane = lax.broadcasted_iota(jnp.int32, (pair, cols), 1)
    row = lax.broadcasted_iota(jnp.int32, (pair, cols), 0)
    is_diag = row == lane % pair
    start = is_diag.astype(jnp.float32)
    square_row = lax.broadcasted_iota(jnp.int32, (cols, cols), 0)
    square_lane = lax.broadcasted_iota(jnp.int32, (cols, cols), 1)
    own_pair = square_row // pair == square_lane // pair
    c_ref[...] = gram_ref[...]
    q_ref[...] = (square_row == square_lane).astype(jnp.float32)

    own_lane = lax.broadcasted_iota(jnp.int32, (pair, LANES), 1)
    table = plan_ref[...]
    table = jnp.concatenate([table + pair * g for g in range(LANES // pair)], axis=1)
    following = pltpu.roll(table, pair - 1, 0)
    partner_of_following = jnp.take_along_axis(table, following, axis=1)

    def sign_of(own, other):
        return jnp.where(own < other, 1.0, -1.0).astype(jnp.float32)

    index_ref[0:pair] = table
    index_ref[pair : 2 * pair] = partner_of_following
    sign_ref[0:pair] = sign_of(own_lane, table)
    sign_ref[pair : 2 * pair] = sign_of(following, partner_of_following)

    def moved(x):
        place = lax.broadcasted_iota(jnp.int32, x.shape, 1)
        is_upper = place % pair < half
        from_own = (place < half) & is_upper
        shifted = ((place // pair == 1) & is_upper) | (place >= cols - half)
        right, left, by_half = pltpu.roll(x, pair, 1), pltpu.roll(x, cols - pair, 1), pltpu.roll(x, half, 1)
        return jnp.where(from_own, x, jnp.where(shifted, by_half, jnp.where(is_upper, right, left)))

    def rows_of(ref, *places):
        return [ref[pl.ds(p, 1), :] for p in places]

    def one_round(round_index, carry):
        kept = jnp.where(own_pair, c_ref[...], 0.0)
        w = kept[0:pair]
        for p in range(1, cols // pair):
            w = w + kept[p * pair : (p + 1) * pair]
        d = jnp.broadcast_to(jnp.sum(jnp.where(is_diag, w, 0.0), axis=0, keepdims=True), (8, cols))
        turned, energies = [], []
        for tile in range(tiles):
            at = slice(tile * LANES, (tile + 1) * LANES)
            state = (w[:, at], start[:, at], d[:, at])

            def steps(k, state):
                first = 2 * k
                index = rows_of(index_ref, first, first + 1, first + pair)
                signs = rows_of(sign_ref, first, first + pair, first + 1)
                return double_step(state, index, signs)

            state = lax.fori_loop(0, n_steps // 2, steps, state)
            if n_steps % 2:
                state = single_step(state, rows_of(index_ref, n_steps - 1), rows_of(sign_ref, n_steps - 1))
            turned.append(state[1])
            energies.append(state[2])
        t = moved(jnp.concatenate(turned, axis=1) if tiles > 1 else turned[0])
        d = jnp.concatenate(energies, axis=1) if tiles > 1 else energies[0]
        energy_ref[...] = moved(d)
        lanes_from = moved(lax.broadcasted_iota(jnp.int32, (8, cols), 1))[0:1] // pair
        whole = jnp.where(square_row // pair == lanes_from, jnp.concatenate([t] * (cols // pair), axis=0), 0.0)
        half_way = dot_full(c_ref[...], whole)
        c_ref[...] = dot_full(whole, half_way, 0, 0)
        q_ref[...] = dot_full(q_ref[...], whole)
        return carry

    lax.fori_loop(0, ROUNDS, one_round, 0)
    place = place_ref[0]
    to_front = lax.rem(cols - place * pair, cols)
    energy_ref[...] = pltpu.roll(energy_ref[...], to_front, 1)
    for d in range(cols // pair):
        rows = q_ref[pl.ds(pl.multiple_of((place ^ d) * pair, pair), pair), :]
        modes_ref[d * pair : (d + 1) * pair] = pltpu.roll(rows, to_front, 1)


def in_vmem(n):
    return [pl.BlockSpec(memory_space=pltpu.VMEM)] * n


def turn_all(gram, plan, place):
    cols = gram.shape[0]
    n_steps, pair = plan.shape
    plan = jnp.concatenate([plan, jnp.arange(pair, dtype=jnp.int32)[None]], axis=0)
    return pl.pallas_call(
        functools.partial(turn_kernel, n_steps),
        out_shape=(
            jax.ShapeDtypeStruct((cols, cols), jnp.float32),
            jax.ShapeDtypeStruct((8, cols), jnp.float32),
        ),
        in_specs=in_vmem(2) + [pl.BlockSpec(memory_space=pltpu.SMEM)],
        out_specs=in_vmem(2),
        scratch_shapes=[
            pltpu.VMEM((cols, cols), jnp.float32),
            pltpu.VMEM((cols, cols), jnp.float32),
            pltpu.VMEM((2 * pair, LANES), jnp.int32),
            pltpu.VMEM((2 * pair, LANES), jnp.float32),
        ],
        compiler_params=pltpu.CompilerParams(vmem_limit_bytes=48 * 1024 * 1024),
        name="all_rounds",
    )(gram, plan, place)


def gram_kernel(place_ref, *refs):
    blocks, gram_ref, whole_ref = refs[:-2], refs[-2], refs[-1]
    pair = blocks[0].shape[0]
    for d, block in enumerate(blocks):
        whole_ref[pl.ds(pl.multiple_of((place_ref[0] ^ d) * pair, pair), pair), :] = block[...]
    whole = whole_ref[...]
    gram_ref[...] = dot_full(whole, whole, 1, 1)


def gram_of(blocks, place):
    pair, cells = blocks[0].shape
    cols = pair * len(blocks)
    return pl.pallas_call(
        gram_kernel,
        out_shape=jax.ShapeDtypeStruct((cols, cols), jnp.float32),
        in_specs=[pl.BlockSpec(memory_space=pltpu.SMEM)] + in_vmem(len(blocks)),
        out_specs=pl.BlockSpec(memory_space=pltpu.VMEM),
        scratch_shapes=[pltpu.VMEM((cols, cells), jnp.float32)],
        name="gram_of_part",
    )(place, *blocks)


def sent(value, axis, toggle):
    return lax.ppermute(value, axis, [(i, i ^ toggle) for i in range(lax.axis_size(axis))])


def tree_sum(values):
    while len(values) > 1:
        values = [a + b for a, b in zip(values[::2], values[1::2])]
    return values[0]


def summed_over_all(x):
    x = x + sent(x, "cell", 1)
    x = tree_sum([x] + [sent(x, "cell", d) for d in range(2, lax.axis_size("cell"), 2)])
    return tree_sum([x] + [sent(x, "blk", d) for d in range(1, lax.axis_size("blk"))])


def on_device(snapshots, plan):
    pair, cells = snapshots.shape
    n_blk = lax.axis_size("blk")
    here = lax.axis_index("blk")
    place = here.astype(jnp.int32)[None]
    part = cells // n_blk

    def part_for(d):
        return lax.dynamic_slice_in_dim(snapshots, (here ^ d) * part, part, 1)

    parts = [part_for(0)] + [sent(part_for(d), "blk", d) for d in range(1, n_blk)]
    blocks = [snapshots] + [sent(snapshots, "blk", d) for d in range(1, n_blk)]
    gram = summed_over_all(gram_of(parts, place))
    modes, energy = turn_all(gram, plan, place)
    rotated = lax.dot_general(
        modes[:, :pair],
        jnp.concatenate(blocks, axis=0),
        (((0,), (0,)), ((), ())),
        precision=lax.Precision.HIGHEST,
    )
    mode_energy = energy[0, :pair] / (cells * lax.axis_size("cell"))
    return rotated * rotated, mode_energy


def solution(mesh):
    return jax.shard_map(
        on_device,
        mesh=mesh,
        in_specs=(P("blk", "cell"), P()),
        out_specs=(P("blk", "cell"), P("blk")),
        check_vma=False,
    )
```

```python
import functools

import jax
import jax.numpy as jnp
from jax import lax
from jax.experimental import pallas as pl
from jax.experimental.pallas import tpu as pltpu
from jax.sharding import PartitionSpec as P

ROUNDS = 7
TINY_SQUARE = 2.0**-78
UP = 2.0**80
FLOOR = 2.0**-124
FLOOR_ROOT = 2.0**-62
LANES = 128


def split3(x):
    high = x.astype(jnp.bfloat16)
    rest = x - high.astype(jnp.float32)
    middle = rest.astype(jnp.bfloat16)
    low = (rest - middle.astype(jnp.float32)).astype(jnp.bfloat16)
    return high, middle, low


def dot_full(a, b, contract_a=1, contract_b=0):
    a0, a1, a2 = split3(a)
    b0, b1, b2 = split3(b)

    def one(x, y):
        return lax.dot_general(
            x, y, (((contract_a,), (contract_b,)), ((), ())), preferred_element_type=jnp.float32
        )

    small = one(a0, b2) + one(a2, b0) + one(a1, b1)
    return one(a0, b0) + ((one(a0, b1) + one(a1, b0)) + small)


def half_angle(twice_cross, spread, sign):
    up_cross, up_spread = twice_cross * UP, spread * UP
    square = spread * spread + twice_cross * twice_cross
    up_square = up_spread * up_spread + up_cross * up_cross
    is_small = square < TINY_SQUARE
    norm_square = jnp.maximum(jnp.where(is_small, up_square, square), FLOOR)
    size = jnp.maximum(jnp.abs(jnp.where(is_small, up_spread, spread)), FLOOR_ROOT)
    half_cross = jnp.where(is_small, up_cross, twice_cross) * (0.5 * sign)
    cross_sign = jnp.where(twice_cross < 0, -sign, sign)
    inverse = lax.rsqrt(norm_square)
    large_square = 0.5 * (size * inverse) + 0.5
    root = lax.rsqrt(large_square)
    large = large_square * root
    small = (half_cross * inverse) * root
    in_order = spread >= 0
    cosine = jnp.where(in_order, large, jnp.abs(small))
    sine = jnp.where(in_order, small, cross_sign * large)
    return cosine, sine


def gather(x, index):
    return jnp.take_along_axis(x, jnp.broadcast_to(index, x.shape), axis=1)


def tall(x, like):
    return jnp.concatenate([x] * (like.shape[0] // x.shape[0]), axis=0)


def turned_by(c, s, x, y):
    return tall(c, x) * x + tall(s, x) * y


def both(wx, tx, wy, ty):
    return jnp.sum(wx * ty + wy * tx, axis=0, keepdims=True)


def new_diagonal(cosine, sine, twice_cross, own, other):
    return (cosine * cosine) * own + (cosine * sine) * twice_cross + (sine * sine) * other


def single_step(state, index, signs):
    w, t, d = state
    (p,) = index
    wp, tp, dp = gather(w, p), gather(t, p), gather(d, p)
    (sign,) = signs
    cross = both(w, t, wp, tp)
    c, s = half_angle(cross, (d - dp) * sign, sign)
    return turned_by(c, s, w, wp), turned_by(c, s, t, tp), new_diagonal(c, s, cross, d, dp)


def double_step(state, index, signs):
    w, t, d = state
    p, q, pq = index
    sign, sign_q, sign_next = signs
    wp, tp, dp = gather(w, p), gather(t, p), gather(d, p)
    wq, tq, dq = gather(w, q), gather(t, q), gather(d, q)
    wpq, tpq, dpq = gather(w, pq), gather(t, pq), gather(d, pq)
    cross = both(w, t, wp, tp)
    cross_q = both(wq, tq, wpq, tpq)
    e00, e01 = both(w, t, wq, tq), both(w, t, wpq, tpq)
    e10, e11 = both(wp, tp, wq, tq), both(wp, tp, wpq, tpq)
    c, s = half_angle(cross, (d - dp) * sign, sign)
    cq, sq = half_angle(cross_q, (dq - dpq) * sign_q, sign_q)
    cross_next = ((c * cq) * e00 + (s * sq) * e11) + ((c * sq) * e01 + (s * cq) * e10)
    d1 = new_diagonal(c, s, cross, d, dp)
    d1q = new_diagonal(cq, sq, cross_q, dq, dpq)
    c1, s1 = half_angle(cross_next, (d1 - d1q) * sign_next, sign_next)
    w1, t1 = turned_by(c, s, w, wp), turned_by(c, s, t, tp)
    w1q, t1q = turned_by(cq, sq, wq, wpq), turned_by(cq, sq, tq, tpq)
    return (
        turned_by(c1, s1, w1, w1q),
        turned_by(c1, s1, t1, t1q),
        new_diagonal(c1, s1, cross_next, d1, d1q),
    )


def turn_kernel(n_steps, n_cells, gram_ref, plan_ref, place_ref, modes_ref, mean_ref, energy_ref, c_ref, q_ref, index_ref, sign_ref):
    cols = gram_ref.shape[0]
    pair = plan_ref.shape[1]
    half = pair // 2
    tiles = cols // LANES
    lane = lax.broadcasted_iota(jnp.int32, (pair, cols), 1)
    row = lax.broadcasted_iota(jnp.int32, (pair, cols), 0)
    is_diag = row == lane % pair
    start = is_diag.astype(jnp.float32)
    square_row = lax.broadcasted_iota(jnp.int32, (cols, cols), 0)
    square_lane = lax.broadcasted_iota(jnp.int32, (cols, cols), 1)
    own_pair = square_row // pair == square_lane // pair
    c_ref[...] = gram_ref[...]
    q_ref[...] = (square_row == square_lane).astype(jnp.float32)

    own_lane = lax.broadcasted_iota(jnp.int32, (pair, LANES), 1)
    table = plan_ref[...]
    table = jnp.concatenate([table + pair * g for g in range(LANES // pair)], axis=1)
    following = pltpu.roll(table, pair - 1, 0)
    partner_of_following = jnp.take_along_axis(table, following, axis=1)

    def sign_of(own, other):
        return jnp.where(own < other, 1.0, -1.0).astype(jnp.float32)

    index_ref[0:pair] = table
    index_ref[pair : 2 * pair] = partner_of_following
    sign_ref[0:pair] = sign_of(own_lane, table)
    sign_ref[pair : 2 * pair] = sign_of(following, partner_of_following)

    def moved(x):
        place = lax.broadcasted_iota(jnp.int32, x.shape, 1)
        is_upper = place % pair < half
        from_own = (place < half) & is_upper
        shifted = ((place // pair == 1) & is_upper) | (place >= cols - half)
        right, left, by_half = pltpu.roll(x, pair, 1), pltpu.roll(x, cols - pair, 1), pltpu.roll(x, half, 1)
        return jnp.where(from_own, x, jnp.where(shifted, by_half, jnp.where(is_upper, right, left)))

    def rows_of(ref, *places):
        return [ref[pl.ds(p, 1), :] for p in places]

    def one_round(round_index, carry):
        kept = jnp.where(own_pair, c_ref[...], 0.0)
        w = kept[0:pair]
        for p in range(1, cols // pair):
            w = w + kept[p * pair : (p + 1) * pair]
        d = jnp.broadcast_to(jnp.sum(jnp.where(is_diag, w, 0.0), axis=0, keepdims=True), (8, cols))
        turned, energies = [], []
        for tile in range(tiles):
            at = slice(tile * LANES, (tile + 1) * LANES)
            state = (w[:, at], start[:, at], d[:, at])

            def steps(k, state):
                first = 2 * k
                index = rows_of(index_ref, first, first + 1, first + pair)
                signs = rows_of(sign_ref, first, first + pair, first + 1)
                return double_step(state, index, signs)

            state = lax.fori_loop(0, n_steps // 2, steps, state)
            if n_steps % 2:
                state = single_step(state, rows_of(index_ref, n_steps - 1), rows_of(sign_ref, n_steps - 1))
            turned.append(state[1])
            energies.append(state[2])
        t = moved(jnp.concatenate(turned, axis=1) if tiles > 1 else turned[0])
        d = jnp.concatenate(energies, axis=1) if tiles > 1 else energies[0]
        energy_ref[...] = moved(d)
        lanes_from = moved(lax.broadcasted_iota(jnp.int32, (8, cols), 1))[0:1] // pair
        whole = jnp.where(square_row // pair == lanes_from, jnp.concatenate([t] * (cols // pair), axis=0), 0.0)
        half_way = dot_full(c_ref[...], whole)
        c_ref[...] = dot_full(whole, half_way, 0, 0)
        q_ref[...] = dot_full(q_ref[...], whole)
        return carry

    lax.fori_loop(0, ROUNDS, one_round, 0)
    place = place_ref[0]
    to_front = lax.rem(cols - place * pair, cols)
    mean_ref[...] = pltpu.roll(energy_ref[...], to_front, 1)[0:1, 0:pair] / n_cells
    for d in range(cols // pair):
        rows = q_ref[pl.ds(pl.multiple_of((place ^ d) * pair, pair), pair), :]
        modes_ref[d * pair : (d + 1) * pair] = pltpu.roll(rows, to_front, 1)[:, 0:pair]


def in_vmem(n):
    return [pl.BlockSpec(memory_space=pltpu.VMEM)] * n


def turn_all(gram, plan, place, n_cells):
    cols = gram.shape[0]
    n_steps, pair = plan.shape
    plan = jnp.concatenate([plan, jnp.arange(pair, dtype=jnp.int32)[None]], axis=0)
    return pl.pallas_call(
        functools.partial(turn_kernel, n_steps, n_cells),
        out_shape=(
            jax.ShapeDtypeStruct((cols, pair), jnp.float32),
            jax.ShapeDtypeStruct((1, pair), jnp.float32),
        ),
        in_specs=in_vmem(2) + [pl.BlockSpec(memory_space=pltpu.SMEM)],
        out_specs=in_vmem(2),
        scratch_shapes=[
            pltpu.VMEM((8, cols), jnp.float32),
            pltpu.VMEM((cols, cols), jnp.float32),
            pltpu.VMEM((cols, cols), jnp.float32),
            pltpu.VMEM((2 * pair, LANES), jnp.int32),
            pltpu.VMEM((2 * pair, LANES), jnp.float32),
        ],
        compiler_params=pltpu.CompilerParams(vmem_limit_bytes=48 * 1024 * 1024),
        name="all_rounds",
    )(gram, plan, place)


def sent(value, axis, toggle):
    return lax.ppermute(value, axis, [(i, i ^ toggle) for i in range(lax.axis_size(axis))])


def tree_sum(values):
    while len(values) > 1:
        values = [a + b for a, b in zip(values[::2], values[1::2])]
    return values[0]


def on_device(snapshots, plan):
    pair, cells = snapshots.shape
    n_blk, n_cell = lax.axis_size("blk"), lax.axis_size("cell")
    here = lax.axis_index("blk")
    place = here.astype(jnp.int32)[None]
    part = cells // n_blk

    def part_for(d):
        return lax.dynamic_slice_in_dim(snapshots, (here ^ d) * part, part, 1)

    parts = jnp.stack([part_for(0)] + [sent(part_for(d), "blk", d) for d in range(1, n_blk)])
    parts = [lax.dynamic_index_in_dim(parts, here ^ q, 0, keepdims=False) for q in range(n_blk)]
    whole = jnp.concatenate(parts, axis=0)
    gram = lax.dot_general(whole, whole, (((1,), (1,)), ((), ())), precision=lax.Precision.HIGHEST)
    gram = gram + sent(gram, "cell", 1)
    gram = tree_sum([gram] + [sent(gram, "blk", d) for d in range(1, n_blk)])
    gram, held = lax.optimization_barrier((gram, snapshots))
    blocks = [snapshots] + [sent(held, "blk", d) for d in range(1, n_blk)]
    gram = tree_sum([gram] + [sent(gram, "cell", d) for d in range(2, n_cell, 2)])
    modes, energy = turn_all(gram, plan, place, cells * n_cell)
    rotated = lax.dot_general(
        modes, jnp.concatenate(blocks, axis=0), (((0,), (0,)), ((), ())), precision=lax.Precision.HIGHEST
    )
    return rotated * rotated, energy.reshape(pair)


def solution(mesh):
    return jax.shard_map(
        on_device,
        mesh=mesh,
        in_specs=(P("blk", "cell"), P()),
        out_specs=(P("blk", "cell"), P("blk")),
        check_vma=False,
    )
```

```python
import functools

import jax
import jax.numpy as jnp
from jax import lax
from jax.experimental import pallas as pl
from jax.experimental.pallas import tpu as pltpu
from jax.sharding import PartitionSpec as P

ROUNDS = 7
TINY_SQUARE = 2.0**-78
UP = 2.0**80
FLOOR = 2.0**-124
FLOOR_ROOT = 2.0**-62
LANES = 128


def split3(x):
    high = x.astype(jnp.bfloat16)
    rest = x - high.astype(jnp.float32)
    middle = rest.astype(jnp.bfloat16)
    low = (rest - middle.astype(jnp.float32)).astype(jnp.bfloat16)
    return high, middle, low


def dot_full(a, b, contract_a=1, contract_b=0):
    a0, a1, a2 = split3(a)
    b0, b1, b2 = split3(b)

    def one(x, y):
        return lax.dot_general(
            x, y, (((contract_a,), (contract_b,)), ((), ())), preferred_element_type=jnp.float32
        )

    small = one(a0, b2) + one(a2, b0) + one(a1, b1)
    return one(a0, b0) + ((one(a0, b1) + one(a1, b0)) + small)


def turning(twice_cross, own, other, sign):
    spread = (own - other) * sign
    up_cross, up_spread = twice_cross * UP, spread * UP
    square = spread * spread + twice_cross * twice_cross
    up_square = (up_spread * up_spread + FLOOR) + up_cross * up_cross
    is_small = square < TINY_SQUARE
    norm_square = jnp.where(is_small, up_square, square)
    size = jnp.maximum(jnp.abs(jnp.where(is_small, up_spread, spread)), FLOOR_ROOT)
    cross = jnp.where(is_small, up_cross, twice_cross) * sign
    half_norm = norm_square * jnp.where(is_small, (0.5 / UP) * sign, 0.5 * sign)
    cross_sign = jnp.where(twice_cross < 0, -sign, sign)
    in_order = spread >= 0
    inverse = lax.rsqrt(norm_square)
    large = size * inverse + 1.0
    small = cross * inverse
    u = jnp.where(in_order, large, jnp.abs(small))
    v = jnp.where(in_order, small, cross_sign * large)
    return u, v, lax.rsqrt(large + large), 0.5 * (own + other) + half_norm * inverse


def gather(x, index):
    return jnp.take_along_axis(x, jnp.broadcast_to(index, x.shape), axis=1)


def tall(x, like):
    return jnp.concatenate([x] * (like.shape[0] // x.shape[0]), axis=0)


def turned_by(c, s, x, y):
    return tall(c, x) * x + tall(s, x) * y


def both(wx, tx, wy, ty):
    return jnp.sum(wx * ty + wy * tx, axis=0, keepdims=True)


def last_step(state, places, sign):
    w, t, d = state
    (wi, ti, di), (wp, tp, dp) = [[gather(x, place) for x in (w, t, d)] for place in places]
    u, v, f, d = turning(both(wi, ti, wp, tp), di, dp, sign)
    return turned_by(u * f, v * f, ti, tp), d


def double_step(state, index, signs):
    w, t, d = state
    p, q, pq = index
    sign, sign_q, sign_next = signs
    wq, tq, dq = gather(w, q), gather(t, q), gather(d, q)
    wpq, tpq, dpq = gather(w, pq), gather(t, pq), gather(d, pq)
    wp, tp, dp = gather(w, p), gather(t, p), gather(d, p)
    u, v, f, d1 = turning(both(w, t, wp, tp), d, dp, sign)
    uq, vq, fq, d1q = turning(both(wq, tq, wpq, tpq), dq, dpq, sign_q)
    e00, e01 = both(w, t, wq, tq), both(w, t, wpq, tpq)
    e10, e11 = both(wp, tp, wq, tq), both(wp, tp, wpq, tpq)
    cross = (f * fq) * (((u * uq) * e00 + (v * vq) * e11) + ((u * vq) * e01 + (v * uq) * e10))
    u1, v1, f1, d2 = turning(cross, d1, d1q, sign_next)
    c, s, cq, sq = u * f, v * f, uq * fq, vq * fq
    c1, s1 = u1 * f1, v1 * f1
    w1, t1 = turned_by(c, s, w, wp), turned_by(c, s, t, tp)
    w1q, t1q = turned_by(cq, sq, wq, wpq), turned_by(cq, sq, tq, tpq)
    return turned_by(c1, s1, w1, w1q), turned_by(c1, s1, t1, t1q), d2


def turn_kernel(n_steps, n_cells, gram_ref, plan_ref, place_ref, modes_ref, mean_ref, energy_ref, c_ref, q_ref, index_ref, sign_ref):
    cols = gram_ref.shape[0]
    pair = plan_ref.shape[1]
    half = pair // 2
    tiles = cols // LANES
    lane = lax.broadcasted_iota(jnp.int32, (pair, cols), 1)
    row = lax.broadcasted_iota(jnp.int32, (pair, cols), 0)
    is_diag = row == lane % pair
    start = is_diag.astype(jnp.float32)
    square_row = lax.broadcasted_iota(jnp.int32, (cols, cols), 0)
    square_lane = lax.broadcasted_iota(jnp.int32, (cols, cols), 1)
    own_pair = square_row // pair == square_lane // pair
    c_ref[...] = gram_ref[...]
    q_ref[...] = (square_row == square_lane).astype(jnp.float32)

    own_lane = lax.broadcasted_iota(jnp.int32, (pair, LANES), 1)
    table = plan_ref[...]
    table = jnp.concatenate([table + pair * g for g in range(LANES // pair)], axis=1)
    following = pltpu.roll(table, pair - 1, 0)
    partner_of_following = jnp.take_along_axis(table, following, axis=1)

    def sign_of(own, other):
        return jnp.where(own < other, 1.0, -1.0).astype(jnp.float32)

    index_ref[0:pair] = table
    index_ref[pair : 2 * pair] = partner_of_following
    sign_ref[0:pair] = sign_of(own_lane, table)
    sign_ref[pair : 2 * pair] = sign_of(following, partner_of_following)

    def moved(x):
        place = lax.broadcasted_iota(jnp.int32, x.shape, 1)
        is_upper = place % pair < half
        from_own = (place < half) & is_upper
        shifted = ((place // pair == 1) & is_upper) | (place >= cols - half)
        right, left, by_half = pltpu.roll(x, pair, 1), pltpu.roll(x, cols - pair, 1), pltpu.roll(x, half, 1)
        return jnp.where(from_own, x, jnp.where(shifted, by_half, jnp.where(is_upper, right, left)))

    def rows_of(ref, *places):
        return [ref[pl.ds(p, 1), :] for p in places]

    arrivals = moved(lax.broadcasted_iota(jnp.int32, (8, cols), 1))
    last = jnp.broadcast_to(table[n_steps - 1 : n_steps], (8, LANES))
    last_places = [arrivals, gather(last, arrivals)] if tiles == 1 else [own_lane[0:8], last]
    last_places = [x[0:1] for x in last_places]
    last_sign = sign_of(*last_places)
    arrivals = arrivals[0:1]

    def sweep():
        kept = jnp.where(own_pair, c_ref[...], 0.0)
        w = kept[0:pair]
        for p in range(1, cols // pair):
            w = w + kept[p * pair : (p + 1) * pair]
        d = jnp.broadcast_to(jnp.sum(jnp.where(is_diag, w, 0.0), axis=0, keepdims=True), (8, cols))
        turned, energies = [], []
        for tile in range(tiles):
            at = slice(tile * LANES, (tile + 1) * LANES)

            def steps(k, state):
                first = 2 * k
                index = rows_of(index_ref, first, first + 1, first + pair)
                signs = rows_of(sign_ref, first, first + pair, first + 1)
                return double_step(state, index, signs)

            begin = (w[:, at], start[:, at], d[:, at])
            state = lax.fori_loop(0, n_steps // 2, steps, begin, unroll=5)
            t, d_tile = last_step(state, last_places, last_sign)
            turned.append(t)
            energies.append(d_tile)
        if tiles == 1:
            t, energy_ref[...] = turned[0], energies[0]
        else:
            t, energy_ref[...] = moved(jnp.concatenate(turned, axis=1)), moved(jnp.concatenate(energies, axis=1))
        whole = jnp.concatenate([t] * (cols // pair), axis=0)
        return jnp.where(square_row // pair == arrivals // pair, whole, 0.0)

    def one_round(round_index, carry):
        whole = sweep()
        half_way = dot_full(c_ref[...], whole)
        c_ref[...] = dot_full(whole, half_way, 0, 0)
        q_ref[...] = dot_full(q_ref[...], whole)
        return carry

    lax.fori_loop(0, ROUNDS - 1, one_round, 0)
    q_ref[...] = dot_full(q_ref[...], sweep())
    place = place_ref[0]
    to_front = lax.rem(cols - place * pair, cols)
    mean_ref[...] = pltpu.roll(energy_ref[...], to_front, 1)[0:1, 0:pair] / n_cells
    for d in range(cols // pair):
        rows = q_ref[pl.ds(pl.multiple_of((place ^ d) * pair, pair), pair), :]
        modes_ref[d * pair : (d + 1) * pair] = pltpu.roll(rows, to_front, 1)[:, 0:pair]


def in_vmem(n):
    return [pl.BlockSpec(memory_space=pltpu.VMEM)] * n


def turn_all(gram, plan, place, n_cells):
    cols = gram.shape[0]
    n_steps, pair = plan.shape
    plan = jnp.concatenate([plan, jnp.arange(pair, dtype=jnp.int32)[None]], axis=0)
    return pl.pallas_call(
        functools.partial(turn_kernel, n_steps, n_cells),
        out_shape=(
            jax.ShapeDtypeStruct((cols, pair), jnp.float32),
            jax.ShapeDtypeStruct((1, pair), jnp.float32),
        ),
        in_specs=in_vmem(2) + [pl.BlockSpec(memory_space=pltpu.SMEM)],
        out_specs=in_vmem(2),
        scratch_shapes=[
            pltpu.VMEM((8, cols), jnp.float32),
            pltpu.VMEM((cols, cols), jnp.float32),
            pltpu.VMEM((cols, cols), jnp.float32),
            pltpu.VMEM((2 * pair, LANES), jnp.int32),
            pltpu.VMEM((2 * pair, LANES), jnp.float32),
        ],
        compiler_params=pltpu.CompilerParams(vmem_limit_bytes=48 * 1024 * 1024),
        name="all_rounds",
    )(gram, plan, place)


def sent(value, axis, toggle):
    return lax.ppermute(value, axis, [(i, i ^ toggle) for i in range(lax.axis_size(axis))])


def tree_sum(values):
    while len(values) > 1:
        values = [a + b for a, b in zip(values[::2], values[1::2])]
    return values[0]


def on_device(snapshots, plan):
    pair, cells = snapshots.shape
    n_blk, n_cell = lax.axis_size("blk"), lax.axis_size("cell")
    here = lax.axis_index("blk")
    place = here.astype(jnp.int32)[None]
    part = cells // n_blk

    def part_for(d):
        return lax.dynamic_slice_in_dim(snapshots, (here ^ d) * part, part, 1)

    parts = jnp.stack([part_for(0)] + [sent(part_for(d), "blk", d) for d in range(1, n_blk)])
    parts = [lax.dynamic_index_in_dim(parts, here ^ q, 0, keepdims=False) for q in range(n_blk)]
    whole = jnp.concatenate(parts, axis=0)
    gram = lax.dot_general(whole, whole, (((1,), (1,)), ((), ())), precision=lax.Precision.HIGHEST)
    gram = gram + sent(gram, "cell", 1)
    gram = tree_sum([gram] + [sent(gram, "blk", d) for d in range(1, n_blk)])
    gram, held = lax.optimization_barrier((gram, snapshots))
    blocks = [snapshots] + [sent(held, "blk", d) for d in range(1, n_blk)]
    gram = tree_sum([gram] + [sent(gram, "cell", d) for d in range(2, n_cell, 2)])
    modes, energy = turn_all(gram, plan, place, cells * n_cell)
    rotated = lax.dot_general(
        modes, jnp.concatenate(blocks, axis=0), (((0,), (0,)), ((), ())), precision=lax.Precision.HIGHEST
    )
    return rotated * rotated, energy.reshape(pair)


def solution(mesh):
    return jax.shard_map(
        on_device,
        mesh=mesh,
        in_specs=(P("blk", "cell"), P()),
        out_specs=(P("blk", "cell"), P("blk")),
        check_vma=False,
    )
```

```python
import functools

import jax
import jax.numpy as jnp
from jax import lax
from jax.experimental import pallas as pl
from jax.experimental.pallas import tpu as pltpu
from jax.sharding import PartitionSpec as P

ROUNDS = 7
TINY_SQUARE = 2.0**-78
UP = 2.0**80
FLOOR = 2.0**-124
FLOOR_ROOT = 2.0**-62
LANES = 128


def split3(x):
    high = x.astype(jnp.bfloat16)
    rest = x - high.astype(jnp.float32)
    middle = rest.astype(jnp.bfloat16)
    low = (rest - middle.astype(jnp.float32)).astype(jnp.bfloat16)
    return high, middle, low


def dot_full(a, b, contract_a=1, contract_b=0):
    a0, a1, a2 = split3(a)
    b0, b1, b2 = split3(b)

    def one(x, y):
        return lax.dot_general(
            x, y, (((contract_a,), (contract_b,)), ((), ())), preferred_element_type=jnp.float32
        )

    small = one(a0, b2) + one(a2, b0) + one(a1, b1)
    return one(a0, b0) + ((one(a0, b1) + one(a1, b0)) + small)


def turning(twice_cross, own, other, sign):
    spread = (own - other) * sign
    up_cross, up_spread = twice_cross * UP, spread * UP
    square = spread * spread + twice_cross * twice_cross
    up_square = (up_spread * up_spread + FLOOR) + up_cross * up_cross
    is_small = square < TINY_SQUARE
    norm_square = jnp.where(is_small, up_square, square)
    size = jnp.maximum(jnp.abs(jnp.where(is_small, up_spread, spread)), FLOOR_ROOT)
    cross = jnp.where(is_small, up_cross, twice_cross) * sign
    half_norm = norm_square * jnp.where(is_small, (0.5 / UP) * sign, 0.5 * sign)
    cross_sign = jnp.where(twice_cross < 0, -sign, sign)
    in_order = spread >= 0
    inverse = lax.rsqrt(norm_square)
    large = size * inverse + 1.0
    small = cross * inverse
    u = jnp.where(in_order, large, jnp.abs(small))
    v = jnp.where(in_order, small, cross_sign * large)
    return u, v, lax.rsqrt(large + large), 0.5 * (own + other) + half_norm * inverse


def gather(x, index):
    return jnp.take_along_axis(x, jnp.broadcast_to(index, x.shape), axis=1)


def tall(x, like):
    return jnp.concatenate([x] * (like.shape[0] // x.shape[0]), axis=0)


def turned_by(c, s, x, y):
    return tall(c, x) * x + tall(s, x) * y


def both(wx, tx, wy, ty):
    return jnp.sum(wx * ty + wy * tx, axis=0, keepdims=True)


def last_step(state, places, sign):
    w, t, d = state
    (wi, ti, di), (wp, tp, dp) = [[gather(x, place) for x in (w, t, d)] for place in places]
    u, v, f, d = turning(both(wi, ti, wp, tp), di, dp, sign)
    return turned_by(u * f, v * f, ti, tp), d


def double_step(state, index, signs):
    w, t, d = state
    p, q, pq = index
    sign, sign_q, sign_next = signs
    wq, tq, dq = gather(w, q), gather(t, q), gather(d, q)
    wpq, tpq, dpq = gather(w, pq), gather(t, pq), gather(d, pq)
    wp, tp, dp = gather(w, p), gather(t, p), gather(d, p)
    u, v, f, d1 = turning(both(w, t, wp, tp), d, dp, sign)
    uq, vq, fq, d1q = turning(both(wq, tq, wpq, tpq), dq, dpq, sign_q)
    e00, e01 = both(w, t, wq, tq), both(w, t, wpq, tpq)
    e10, e11 = both(wp, tp, wq, tq), both(wp, tp, wpq, tpq)
    cross = (f * fq) * (((u * uq) * e00 + (v * vq) * e11) + ((u * vq) * e01 + (v * uq) * e10))
    u1, v1, f1, d2 = turning(cross, d1, d1q, sign_next)
    c, s, cq, sq = u * f, v * f, uq * fq, vq * fq
    c1, s1 = u1 * f1, v1 * f1
    w1, t1 = turned_by(c, s, w, wp), turned_by(c, s, t, tp)
    w1q, t1q = turned_by(cq, sq, wq, wpq), turned_by(cq, sq, tq, tpq)
    return turned_by(c1, s1, w1, w1q), turned_by(c1, s1, t1, t1q), d2


def unpacked(x):
    cols = x.shape[1]
    half, quarter = cols // 2, cols // 4
    low = x[half:]
    upper = jnp.concatenate([x[:half], low, pltpu.roll(low, 3 * quarter, 1)], axis=0)
    row = lax.broadcasted_iota(jnp.int32, (cols, cols), 0) // quarter
    lane = lax.broadcasted_iota(jnp.int32, (cols, cols), 1) // quarter
    return jnp.where(lane >= row, upper, upper.T)


def turn_kernel(n_steps, n_cells, gram_ref, plan_ref, place_ref, modes_ref, mean_ref, energy_ref, c_ref, q_ref, index_ref, sign_ref):
    cols = gram_ref.shape[1]
    pair = plan_ref.shape[1]
    half = pair // 2
    tiles = cols // LANES
    lane = lax.broadcasted_iota(jnp.int32, (pair, cols), 1)
    row = lax.broadcasted_iota(jnp.int32, (pair, cols), 0)
    is_diag = row == lane % pair
    start = is_diag.astype(jnp.float32)
    square_row = lax.broadcasted_iota(jnp.int32, (cols, cols), 0)
    square_lane = lax.broadcasted_iota(jnp.int32, (cols, cols), 1)
    own_pair = square_row // pair == square_lane // pair
    c_ref[...] = unpacked(gram_ref[...])
    q_ref[...] = (square_row == square_lane).astype(jnp.float32)

    own_lane = lax.broadcasted_iota(jnp.int32, (pair, LANES), 1)
    table = plan_ref[...]
    table = jnp.concatenate([table + pair * g for g in range(LANES // pair)], axis=1)
    following = pltpu.roll(table, pair - 1, 0)
    partner_of_following = jnp.take_along_axis(table, following, axis=1)

    def sign_of(own, other):
        return jnp.where(own < other, 1.0, -1.0).astype(jnp.float32)

    index_ref[0:pair] = table
    index_ref[pair : 2 * pair] = partner_of_following
    sign_ref[0:pair] = sign_of(own_lane, table)
    sign_ref[pair : 2 * pair] = sign_of(following, partner_of_following)

    def moved(x):
        place = lax.broadcasted_iota(jnp.int32, x.shape, 1)
        is_upper = place % pair < half
        from_own = (place < half) & is_upper
        shifted = ((place // pair == 1) & is_upper) | (place >= cols - half)
        right, left, by_half = pltpu.roll(x, pair, 1), pltpu.roll(x, cols - pair, 1), pltpu.roll(x, half, 1)
        return jnp.where(from_own, x, jnp.where(shifted, by_half, jnp.where(is_upper, right, left)))

    def rows_of(ref, *places):
        return [ref[pl.ds(p, 1), :] for p in places]

    arrivals = moved(lax.broadcasted_iota(jnp.int32, (8, cols), 1))
    last = jnp.broadcast_to(table[n_steps - 1 : n_steps], (8, LANES))
    last_places = [arrivals, gather(last, arrivals)] if tiles == 1 else [own_lane[0:8], last]
    last_places = [x[0:1] for x in last_places]
    last_sign = sign_of(*last_places)
    arrivals = arrivals[0:1]

    def sweep():
        kept = jnp.where(own_pair, c_ref[...], 0.0)
        w = kept[0:pair]
        for p in range(1, cols // pair):
            w = w + kept[p * pair : (p + 1) * pair]
        d = jnp.broadcast_to(jnp.sum(jnp.where(is_diag, w, 0.0), axis=0, keepdims=True), (8, cols))
        turned, energies = [], []
        for tile in range(tiles):
            at = slice(tile * LANES, (tile + 1) * LANES)

            def steps(k, state):
                first = 2 * k
                index = rows_of(index_ref, first, first + 1, first + pair)
                signs = rows_of(sign_ref, first, first + pair, first + 1)
                return double_step(state, index, signs)

            begin = (w[:, at], start[:, at], d[:, at])
            state = lax.fori_loop(0, n_steps // 2, steps, begin, unroll=5)
            t, d_tile = last_step(state, last_places, last_sign)
            turned.append(t)
            energies.append(d_tile)
        if tiles == 1:
            t, energy_ref[...] = turned[0], energies[0]
        else:
            t, energy_ref[...] = moved(jnp.concatenate(turned, axis=1)), moved(jnp.concatenate(energies, axis=1))
        whole = jnp.concatenate([t] * (cols // pair), axis=0)
        return jnp.where(square_row // pair == arrivals // pair, whole, 0.0)

    def one_round(round_index, carry):
        whole = sweep()
        half_way = dot_full(c_ref[...], whole)
        c_ref[...] = dot_full(whole, half_way, 0, 0)
        q_ref[...] = dot_full(q_ref[...], whole)
        return carry

    lax.fori_loop(0, ROUNDS - 1, one_round, 0)
    q_ref[...] = dot_full(q_ref[...], sweep())
    place = place_ref[0]
    to_front = lax.rem(cols - place * pair, cols)
    mean_ref[...] = pltpu.roll(energy_ref[...], to_front, 1)[0:1, 0:pair] / n_cells
    for d in range(cols // pair):
        rows = q_ref[pl.ds(pl.multiple_of((place ^ d) * pair, pair), pair), :]
        modes_ref[d * pair : (d + 1) * pair] = pltpu.roll(rows, to_front, 1)[:, 0:pair]


def in_vmem(n):
    return [pl.BlockSpec(memory_space=pltpu.VMEM)] * n


def turn_all(gram, plan, place, n_cells):
    cols = gram.shape[1]
    n_steps, pair = plan.shape
    plan = jnp.concatenate([plan, jnp.arange(pair, dtype=jnp.int32)[None]], axis=0)
    return pl.pallas_call(
        functools.partial(turn_kernel, n_steps, n_cells),
        out_shape=(
            jax.ShapeDtypeStruct((cols, pair), jnp.float32),
            jax.ShapeDtypeStruct((1, pair), jnp.float32),
        ),
        in_specs=in_vmem(2) + [pl.BlockSpec(memory_space=pltpu.SMEM)],
        out_specs=in_vmem(2),
        scratch_shapes=[
            pltpu.VMEM((8, cols), jnp.float32),
            pltpu.VMEM((cols, cols), jnp.float32),
            pltpu.VMEM((cols, cols), jnp.float32),
            pltpu.VMEM((2 * pair, LANES), jnp.int32),
            pltpu.VMEM((2 * pair, LANES), jnp.float32),
        ],
        compiler_params=pltpu.CompilerParams(vmem_limit_bytes=48 * 1024 * 1024),
        name="all_rounds",
    )(gram, plan, place)


def sent(value, axis, toggle):
    return lax.ppermute(value, axis, [(i, i ^ toggle) for i in range(lax.axis_size(axis))])


def tree_sum(values):
    while len(values) > 1:
        values = [a + b for a, b in zip(values[::2], values[1::2])]
    return values[0]


def packed(gram):
    cols = gram.shape[0]
    half, three = cols // 2, cols // 4 * 3
    corner = jnp.concatenate([gram[three:, three:], jnp.zeros((cols - three, half - (cols - three)), gram.dtype)], axis=1)
    return jnp.concatenate([gram[:half], jnp.concatenate([corner, gram[half:three, half:]], axis=1)], axis=0)


def on_device(snapshots, plan):
    pair, cells = snapshots.shape
    n_blk, n_cell = lax.axis_size("blk"), lax.axis_size("cell")
    here = lax.axis_index("blk")
    place = here.astype(jnp.int32)[None]
    part = cells // n_blk

    def part_for(d):
        return lax.dynamic_slice_in_dim(snapshots, (here ^ d) * part, part, 1)

    parts = jnp.stack([part_for(0)] + [sent(part_for(d), "blk", d) for d in range(1, n_blk)])
    parts = [lax.dynamic_index_in_dim(parts, here ^ q, 0, keepdims=False) for q in range(n_blk)]
    whole = jnp.concatenate(parts, axis=0)
    gram = lax.dot_general(whole, whole, (((1,), (1,)), ((), ())), precision=lax.Precision.HIGHEST)
    gram = packed(gram)
    gram = gram + sent(gram, "cell", 1)
    gram = tree_sum([gram] + [sent(gram, "blk", d) for d in range(1, n_blk)])
    gram, held = lax.optimization_barrier((gram, snapshots))
    blocks = [snapshots] + [sent(held, "blk", d) for d in range(1, n_blk)]
    gram = tree_sum([gram] + [sent(gram, "cell", d) for d in range(2, n_cell, 2)])
    modes, energy = turn_all(gram, plan, place, cells * n_cell)
    rotated = lax.dot_general(
        modes, jnp.concatenate(blocks, axis=0), (((0,), (0,)), ((), ())), precision=lax.Precision.HIGH
    )
    return rotated * rotated, energy.reshape(pair)


def solution(mesh):
    return jax.shard_map(
        on_device,
        mesh=mesh,
        in_specs=(P("blk", "cell"), P()),
        out_specs=(P("blk", "cell"), P("blk")),
        check_vma=False,
    )
```

```python
import functools

import jax
import jax.numpy as jnp
from jax import lax
from jax.experimental import pallas as pl
from jax.experimental.pallas import tpu as pltpu
from jax.sharding import PartitionSpec as P

ROUNDS = 7
TINY_SQUARE = 2.0**-78
UP = 2.0**80
FLOOR = 2.0**-124
FLOOR_ROOT = 2.0**-62
LANES = 128


def split3(x):
    high = x.astype(jnp.bfloat16)
    rest = x - high.astype(jnp.float32)
    middle = rest.astype(jnp.bfloat16)
    low = (rest - middle.astype(jnp.float32)).astype(jnp.bfloat16)
    return high, middle, low


def dot_full(a, b, contract_a=1, contract_b=0):
    a0, a1, a2 = split3(a)
    b0, b1, b2 = split3(b)

    def one(x, y):
        return lax.dot_general(
            x, y, (((contract_a,), (contract_b,)), ((), ())), preferred_element_type=jnp.float32
        )

    small = one(a0, b2) + one(a2, b0) + one(a1, b1)
    return one(a0, b0) + ((one(a0, b1) + one(a1, b0)) + small)


def turning(twice_cross, own, other, sign):
    spread = (own - other) * sign
    up_cross, up_spread = twice_cross * UP, spread * UP
    square = spread * spread + twice_cross * twice_cross
    up_square = (up_spread * up_spread + FLOOR) + up_cross * up_cross
    is_small = square < TINY_SQUARE
    norm_square = jnp.where(is_small, up_square, square)
    size = jnp.maximum(jnp.abs(jnp.where(is_small, up_spread, spread)), FLOOR_ROOT)
    cross = jnp.where(is_small, up_cross, twice_cross) * sign
    half_norm = norm_square * jnp.where(is_small, (0.5 / UP) * sign, 0.5 * sign)
    cross_sign = jnp.where(twice_cross < 0, -sign, sign)
    in_order = spread >= 0
    inverse = lax.rsqrt(norm_square)
    large = size * inverse + 1.0
    double = (size + size) * inverse + 2.0
    small = cross * inverse
    u = jnp.where(in_order, large, jnp.abs(small))
    v = jnp.where(in_order, small, cross_sign * large)
    return u, v, lax.rsqrt(double), 0.5 * (own + other) + half_norm * inverse


def gather(x, index):
    return jnp.take_along_axis(x, jnp.broadcast_to(index, x.shape), axis=1)


def tall(x, like):
    return jnp.concatenate([x] * (like.shape[0] // x.shape[0]), axis=0)


def turned_by(c, s, x, y):
    return tall(c, x) * x + tall(s, x) * y


def product(x, y):
    return jnp.sum(x * y, axis=0, keepdims=True)


def last_step(state, places, sign):
    z, t, d = state
    (zi, ti, di), (zp, tp, dp) = [[gather(x, place) for x in (z, t, d)] for place in places]
    u, v, f, d = turning(product(zi, zp), di, dp, sign)
    return turned_by(u * f, v * f, ti, tp), d


def double_step(state, index_tile, sign_tile):
    z, zc, d = state
    p, q, pq = [index_tile[k : k + 1] for k in range(3)]
    sign, sign_q, sign_next = [sign_tile[k : k + 1] for k in range(3)]
    zp, zq, zpq = gather(z, p), gather(z, q), gather(z, pq)
    diagonals = jnp.take_along_axis(d, index_tile, axis=1)
    dp, dq, dpq = [jnp.broadcast_to(diagonals[k : k + 1], d.shape) for k in range(3)]
    zcq, zcp, zcpq = gather(zc, q), gather(zc, p), gather(zc, pq)
    u, v, f, d1 = turning(product(z, zp), d, dp, sign)
    uq, vq, fq, d1q = turning(product(zq, zpq), dq, dpq, sign_q)
    e00, e11 = product(z, zq), product(zp, zpq)
    e01, e10 = product(zc, zpq), product(zp, zcq)
    cross = (f * fq) * (((u * uq) * e00 + (v * vq) * e11) + ((u * vq) * e01 + (v * uq) * e10))
    u1, v1, f1, d2 = turning(cross, d1, d1q, sign_next)
    c, s, cq, sq = u * f, v * f, uq * fq, vq * fq
    c1, s1 = u1 * f1, v1 * f1
    z1, zc1 = turned_by(c, s, z, zcp), turned_by(c, s, zc, zp)
    zq1, zcq1 = turned_by(cq, sq, zq, zcpq), turned_by(cq, sq, zcq, zpq)
    return turned_by(c1, s1, z1, zcq1), turned_by(c1, s1, zc1, zq1), d2


def moved(x, pair):
    cols, half = x.shape[1], pair // 2
    place = lax.broadcasted_iota(jnp.int32, x.shape, 1)
    is_upper = place % pair < half
    from_own = (place < half) & is_upper
    shifted = ((place // pair == 1) & is_upper) | (place >= cols - half)
    right, left, by_half = pltpu.roll(x, pair, 1), pltpu.roll(x, cols - pair, 1), pltpu.roll(x, half, 1)
    return jnp.where(from_own, x, jnp.where(shifted, by_half, jnp.where(is_upper, right, left)))


def unpacked(x):
    cols = x.shape[1]
    half, quarter = cols // 2, cols // 4
    low = x[half:]
    upper = jnp.concatenate([x[:half], low, pltpu.roll(low, 3 * quarter, 1)], axis=0)
    row = lax.broadcasted_iota(jnp.int32, (cols, cols), 0) // quarter
    lane = lax.broadcasted_iota(jnp.int32, (cols, cols), 1) // quarter
    return jnp.where(lane >= row, upper, upper.T)


def sign_of(own, other):
    return jnp.where(own < other, 1.0, -1.0).astype(jnp.float32)


def table_kernel(plan_ref, index_ref, sign_ref, table_ref):
    pair = plan_ref.shape[1]
    doubles = pair // 2
    table = plan_ref[...]
    table_ref[...] = jnp.concatenate([table + pair * g for g in range(LANES // pair)], axis=1)
    first = table_ref[pl.ds(0, doubles, stride=2), :]
    second = table_ref[pl.ds(1, doubles, stride=2), :]
    own = lax.broadcasted_iota(jnp.int32, (doubles, LANES), 1)
    first_of_second = jnp.take_along_axis(first, second, axis=1)
    around = jnp.take_along_axis(second, first, axis=1)
    least = own
    reach = 1
    while reach < doubles:
        least = jnp.minimum(least, jnp.take_along_axis(least, around, axis=1))
        around = jnp.take_along_axis(around, around, axis=1)
        reach *= 2
    colour = sign_of(least, jnp.take_along_axis(least, first, axis=1))
    lower = sign_of(own, first)
    is_last = lax.broadcasted_iota(jnp.int32, (doubles, LANES), 0) == doubles - 1
    colour = jnp.where(is_last, lower, colour)
    signs = [lower, sign_of(second, first_of_second), sign_of(own, second), colour]
    for k in range(doubles):
        at = slice(k, k + 1)
        index_ref[k] = jnp.concatenate([first[at], second[at]] + [first_of_second[at]] * 6, axis=0)
        sign_ref[k] = jnp.concatenate([x[at] for x in signs] + [lower[at]] * 4, axis=0)


def turn_kernel(n_cells, gram_ref, index_ref, sign_ref, place_ref, modes_ref, mean_ref, energy_ref, c_ref, q_ref):
    cols = gram_ref.shape[1]
    doubles = index_ref.shape[0]
    pair = 2 * doubles
    tiles = cols // LANES
    square_row = lax.broadcasted_iota(jnp.int32, (cols, cols), 0)
    square_lane = lax.broadcasted_iota(jnp.int32, (cols, cols), 1)
    own_pair = square_row // pair == square_lane // pair
    is_diag = (square_row == square_lane % pair)[0:pair]
    start = jnp.where(is_diag, 2.0, 0.0)
    c_ref[...] = unpacked(gram_ref[...])
    q_ref[...] = (square_row == square_lane).astype(jnp.float32)

    arrivals = moved(lax.broadcasted_iota(jnp.int32, (8, cols), 1), pair)
    last = jnp.broadcast_to(index_ref[doubles - 1][0:1], (8, LANES))
    if tiles == 1:
        last_places = [arrivals, gather(last, arrivals)]
    else:
        last_places = [lax.broadcasted_iota(jnp.int32, (8, LANES), 1), last]
    last_places = [x[0:1] for x in last_places]
    last_sign = sign_of(*last_places)
    arrivals = arrivals[0:1]

    def colour_of(k):
        return sign_ref[k][3:4]

    def sweep():
        kept = jnp.where(own_pair, c_ref[...], 0.0)
        w = kept[0:pair]
        for p in range(1, cols // pair):
            w = w + kept[p * pair : (p + 1) * pair]
        d = jnp.broadcast_to(jnp.sum(jnp.where(is_diag, w, 0.0), axis=0, keepdims=True), (8, cols))
        turned, energies = [], []
        for tile in range(tiles):
            at = slice(tile * LANES, (tile + 1) * LANES)
            held = colour_of(0) > 0
            z, zc = jnp.where(held, w[:, at], start[:, at]), jnp.where(held, start[:, at], w[:, at])
            d_tile = d[:, at]
            for k in range(doubles - 1):
                z, zc, d_tile = double_step((z, zc, d_tile), index_ref[k], sign_ref[k])
                same = colour_of(k) * colour_of(k + 1) > 0
                z, zc = jnp.where(same, z, zc), jnp.where(same, zc, z)
            t = jnp.where(colour_of(doubles - 1) > 0, zc, z)
            t, d_tile = last_step((z, t, d_tile), last_places, last_sign)
            turned.append(t)
            energies.append(d_tile)
        if tiles == 1:
            t, energy_ref[...] = turned[0], energies[0]
        else:
            energy_ref[...] = moved(jnp.concatenate(energies, axis=1), pair)
            t = moved(jnp.concatenate(turned, axis=1), pair)
        whole = jnp.concatenate([0.5 * t] * (cols // pair), axis=0)
        return jnp.where(square_row // pair == arrivals // pair, whole, 0.0)

    def one_round(round_index, carry):
        whole = sweep()
        half_way = dot_full(c_ref[...], whole)
        c_ref[...] = dot_full(whole, half_way, 0, 0)
        q_ref[...] = dot_full(q_ref[...], whole)
        return carry

    lax.fori_loop(0, ROUNDS - 1, one_round, 0)
    q_ref[...] = dot_full(q_ref[...], sweep())
    place = place_ref[0]
    to_front = lax.rem(cols - place * pair, cols)
    mean_ref[...] = pltpu.roll(energy_ref[...], to_front, 1)[0:1, 0:pair] / n_cells
    for d in range(cols // pair):
        rows = q_ref[pl.ds(pl.multiple_of((place ^ d) * pair, pair), pair), :]
        modes_ref[d * pair : (d + 1) * pair] = pltpu.roll(rows, to_front, 1)[:, 0:pair]


def in_vmem(n):
    return [pl.BlockSpec(memory_space=pltpu.VMEM)] * n


def tables_of(plan):
    n_steps, pair = plan.shape
    plan = jnp.concatenate([plan, jnp.arange(pair, dtype=jnp.int32)[None]], axis=0)
    shape = ((n_steps + 1) // 2, 8, LANES)
    return pl.pallas_call(
        table_kernel,
        out_shape=(jax.ShapeDtypeStruct(shape, jnp.int32), jax.ShapeDtypeStruct(shape, jnp.float32)),
        in_specs=in_vmem(1),
        out_specs=in_vmem(2),
        scratch_shapes=[pltpu.VMEM((n_steps + 1, LANES), jnp.int32)],
        name="step_tables",
    )(plan)


def turn_all(gram, tables, place, n_cells):
    cols = gram.shape[1]
    pair = 2 * tables[0].shape[0]
    return pl.pallas_call(
        functools.partial(turn_kernel, n_cells),
        out_shape=(
            jax.ShapeDtypeStruct((cols, pair), jnp.float32),
            jax.ShapeDtypeStruct((1, pair), jnp.float32),
        ),
        in_specs=in_vmem(3) + [pl.BlockSpec(memory_space=pltpu.SMEM)],
        out_specs=in_vmem(2),
        scratch_shapes=[
            pltpu.VMEM((8, cols), jnp.float32),
            pltpu.VMEM((cols, cols), jnp.float32),
            pltpu.VMEM((cols, cols), jnp.float32),
        ],
        compiler_params=pltpu.CompilerParams(vmem_limit_bytes=48 * 1024 * 1024),
        name="all_rounds",
    )(gram, *tables, place)


def sent(value, axis, toggle):
    return lax.ppermute(value, axis, [(i, i ^ toggle) for i in range(lax.axis_size(axis))])


def tree_sum(values):
    while len(values) > 1:
        values = [a + b for a, b in zip(values[::2], values[1::2])]
    return values[0]


def packed(gram):
    cols = gram.shape[0]
    half, three = cols // 2, cols // 4 * 3
    corner = jnp.concatenate([gram[three:, three:], jnp.zeros((cols - three, half - (cols - three)), gram.dtype)], axis=1)
    return jnp.concatenate([gram[:half], jnp.concatenate([corner, gram[half:three, half:]], axis=1)], axis=0)


def on_device(snapshots, plan):
    pair, cells = snapshots.shape
    n_blk, n_cell = lax.axis_size("blk"), lax.axis_size("cell")
    here = lax.axis_index("blk")
    place = here.astype(jnp.int32)[None]
    part = cells // n_blk

    def part_for(d):
        return lax.dynamic_slice_in_dim(snapshots, (here ^ d) * part, part, 1)

    parts = jnp.stack([part_for(0)] + [sent(part_for(d), "blk", d) for d in range(1, n_blk)])
    parts = [lax.dynamic_index_in_dim(parts, here ^ q, 0, keepdims=False) for q in range(n_blk)]
    tables, parts = lax.optimization_barrier((tables_of(plan), parts))
    whole = jnp.concatenate(parts, axis=0)
    gram = lax.dot_general(whole, whole, (((1,), (1,)), ((), ())), precision=lax.Precision.HIGHEST)
    gram = packed(gram)
    gram = gram + sent(gram, "cell", 1)
    gram = tree_sum([gram] + [sent(gram, "blk", d) for d in range(1, n_blk)])
    gram, held = lax.optimization_barrier((gram, snapshots))
    blocks = [snapshots] + [sent(held, "blk", d) for d in range(1, n_blk)]
    gram = tree_sum([gram] + [sent(gram, "cell", d) for d in range(2, n_cell, 2)])
    modes, energy = turn_all(gram, tables, place, cells * n_cell)
    rotated = lax.dot_general(
        modes, jnp.concatenate(blocks, axis=0), (((0,), (0,)), ((), ())), precision=lax.Precision.HIGH
    )
    return rotated * rotated, energy.reshape(pair)


def solution(mesh):
    return jax.shard_map(
        on_device,
        mesh=mesh,
        in_specs=(P("blk", "cell"), P()),
        out_specs=(P("blk", "cell"), P("blk")),
        check_vma=False,
    )
```

```python
import functools

import jax
import jax.numpy as jnp
from jax import lax
from jax.experimental import pallas as pl
from jax.experimental.pallas import tpu as pltpu
from jax.sharding import PartitionSpec as P

ROUNDS = 7
TINY_SQUARE = 2.0**-78
UP = 2.0**80
FLOOR = 2.0**-124
FLOOR_ROOT = 2.0**-62
LANES = 128


def split3(x):
    high = x.astype(jnp.bfloat16)
    rest = x - high.astype(jnp.float32)
    middle = rest.astype(jnp.bfloat16)
    low = (rest - middle.astype(jnp.float32)).astype(jnp.bfloat16)
    return high, middle, low


def dot_full(a, b, contract_a=1, contract_b=0):
    a0, a1, a2 = split3(a)
    b0, b1, b2 = split3(b)

    def one(x, y):
        return lax.dot_general(
            x, y, (((contract_a,), (contract_b,)), ((), ())), preferred_element_type=jnp.float32
        )

    small = one(a0, b2) + one(a2, b0) + one(a1, b1)
    return one(a0, b0) + ((one(a0, b1) + one(a1, b0)) + small)


def turning(twice_cross, own, other, sign):
    spread = (own - other) * sign
    up_cross, up_spread = twice_cross * UP, spread * UP
    square = spread * spread + twice_cross * twice_cross
    up_square = (up_spread * up_spread + FLOOR) + up_cross * up_cross
    is_small = square < TINY_SQUARE
    norm_square = jnp.where(is_small, up_square, square)
    size = jnp.maximum(jnp.abs(jnp.where(is_small, up_spread, spread)), FLOOR_ROOT)
    cross = jnp.where(is_small, up_cross, twice_cross) * sign
    half_norm = norm_square * jnp.where(is_small, (0.5 / UP) * sign, 0.5 * sign)
    cross_sign = jnp.where(twice_cross < 0, -sign, sign)
    in_order = spread >= 0
    inverse = lax.rsqrt(norm_square)
    large = size * inverse + 1.0
    double = (size + size) * inverse + 2.0
    small = cross * inverse
    u = jnp.where(in_order, large, jnp.abs(small))
    v = jnp.where(in_order, small, cross_sign * large)
    return u, v, lax.rsqrt(double), 0.5 * (own + other) + half_norm * inverse


def gather(x, index):
    return jnp.take_along_axis(x, jnp.broadcast_to(index, x.shape), axis=1)


def tall(x, like):
    return jnp.concatenate([x] * (like.shape[0] // x.shape[0]), axis=0)


def turned_by(c, s, x, y):
    return tall(c, x) * x + tall(s, x) * y


def product(x, y):
    return jnp.sum(x * y, axis=0, keepdims=True)


def last_step(state, places, sign):
    z, t, d = state
    (zi, ti, di), (zp, tp, dp) = [[gather(x, place) for x in (z, t, d)] for place in places]
    u, v, f, d = turning(product(zi, zp), di, dp, sign)
    return turned_by(u * f, v * f, ti, tp), d


def double_step(state, index_tile, sign_tile, same):
    z, zc, d = state
    p, q, pq = [index_tile[k : k + 1] for k in range(3)]
    sign, sign_q, sign_next = [sign_tile[k : k + 1] for k in range(3)]
    zp, zq, zpq = gather(z, p), gather(z, q), gather(z, pq)
    diagonals = jnp.take_along_axis(d, index_tile, axis=1)
    dp, dq, dpq = [jnp.broadcast_to(diagonals[k : k + 1], d.shape) for k in range(3)]
    zcq, zcp, zcpq = gather(zc, q), gather(zc, p), gather(zc, pq)
    u, v, f, d1 = turning(product(z, zp), d, dp, sign)
    uq, vq, fq, d1q = turning(product(zq, zpq), dq, dpq, sign_q)
    e00, e11 = product(z, zq), product(zp, zpq)
    e01, e10 = product(zc, zpq), product(zp, zcq)
    cross = (f * fq) * (((u * uq) * e00 + (v * vq) * e11) + ((u * vq) * e01 + (v * uq) * e10))
    u1, v1, f1, d2 = turning(cross, d1, d1q, sign_next)
    c, s, cq, sq = u * f, v * f, uq * fq, vq * fq
    z1, zc1 = turned_by(c, s, z, zcp), turned_by(c, s, zc, zp)
    zq1, zcq1 = turned_by(cq, sq, zq, zcpq), turned_by(cq, sq, zcq, zpq)
    own, other = jnp.where(same, z1, zc1), jnp.where(same, zcq1, zq1)
    own_c, other_c = jnp.where(same, zc1, z1), jnp.where(same, zq1, zcq1)
    f1 = tall(f1, z)
    return f1 * turned_by(u1, v1, own, other), f1 * turned_by(u1, v1, own_c, other_c), d2


def moved(x, pair):
    cols, half = x.shape[1], pair // 2
    place = lax.broadcasted_iota(jnp.int32, x.shape, 1)
    is_upper = place % pair < half
    from_own = (place < half) & is_upper
    shifted = ((place // pair == 1) & is_upper) | (place >= cols - half)
    right, left, by_half = pltpu.roll(x, pair, 1), pltpu.roll(x, cols - pair, 1), pltpu.roll(x, half, 1)
    return jnp.where(from_own, x, jnp.where(shifted, by_half, jnp.where(is_upper, right, left)))


def unpacked(x):
    cols = x.shape[1]
    half, quarter = cols // 2, cols // 4
    low = x[half:]
    upper = jnp.concatenate([x[:half], low, pltpu.roll(low, 3 * quarter, 1)], axis=0)
    row = lax.broadcasted_iota(jnp.int32, (cols, cols), 0) // quarter
    lane = lax.broadcasted_iota(jnp.int32, (cols, cols), 1) // quarter
    return jnp.where(lane >= row, upper, upper.T)


def sign_of(own, other):
    return jnp.where(own < other, 1.0, -1.0).astype(jnp.float32)


def table_kernel(plan_ref, index_ref, sign_ref, table_ref):
    pair = plan_ref.shape[1]
    doubles = pair // 2
    table = plan_ref[...]
    table_ref[...] = jnp.concatenate([table + pair * g for g in range(LANES // pair)], axis=1)
    first = table_ref[pl.ds(0, doubles, stride=2), :]
    second = table_ref[pl.ds(1, doubles, stride=2), :]
    own = lax.broadcasted_iota(jnp.int32, (doubles, LANES), 1)
    first_of_second = jnp.take_along_axis(first, second, axis=1)
    around = jnp.take_along_axis(second, first, axis=1)
    least = own
    reach = 1
    while reach < doubles:
        least = jnp.minimum(least, jnp.take_along_axis(least, around, axis=1))
        around = jnp.take_along_axis(around, around, axis=1)
        reach *= 2
    colour = sign_of(least, jnp.take_along_axis(least, first, axis=1))
    lower = sign_of(own, first)
    is_last = lax.broadcasted_iota(jnp.int32, (doubles, LANES), 0) == doubles - 1
    colour = jnp.where(is_last, lower, colour)
    signs = [lower, sign_of(second, first_of_second), sign_of(own, second), colour]
    for k in range(doubles):
        at = slice(k, k + 1)
        index_ref[k] = jnp.concatenate([first[at], second[at]] + [first_of_second[at]] * 6, axis=0)
        sign_ref[k] = jnp.concatenate([x[at] for x in signs] + [lower[at]] * 4, axis=0)


def turn_kernel(n_cells, gram_ref, index_ref, sign_ref, place_ref, modes_ref, mean_ref, energy_ref, c_ref, q_ref):
    cols = gram_ref.shape[1]
    doubles = index_ref.shape[0]
    pair = 2 * doubles
    tiles = cols // LANES
    square_row = lax.broadcasted_iota(jnp.int32, (cols, cols), 0)
    square_lane = lax.broadcasted_iota(jnp.int32, (cols, cols), 1)
    own_pair = square_row // pair == square_lane // pair
    is_diag = (square_row == square_lane % pair)[0:pair]
    start = jnp.where(is_diag, 2.0, 0.0)
    c_ref[...] = unpacked(gram_ref[...])
    q_ref[...] = (square_row == square_lane).astype(jnp.float32)

    arrivals = moved(lax.broadcasted_iota(jnp.int32, (8, cols), 1), pair)
    last = jnp.broadcast_to(index_ref[doubles - 1][0:1], (8, LANES))
    if tiles == 1:
        last_places = [arrivals, gather(last, arrivals)]
    else:
        last_places = [lax.broadcasted_iota(jnp.int32, (8, LANES), 1), last]
    last_places = [x[0:1] for x in last_places]
    last_sign = sign_of(*last_places)
    arrivals = arrivals[0:1]

    def colour_of(k):
        return sign_ref[k][3:4]

    def sweep():
        kept = jnp.where(own_pair, c_ref[...], 0.0)
        w = kept[0:pair]
        for p in range(1, cols // pair):
            w = w + kept[p * pair : (p + 1) * pair]
        d = jnp.broadcast_to(jnp.sum(jnp.where(is_diag, w, 0.0), axis=0, keepdims=True), (8, cols))
        turned, energies = [], []
        for tile in range(tiles):
            at = slice(tile * LANES, (tile + 1) * LANES)
            held = colour_of(0) > 0
            z, zc = jnp.where(held, w[:, at], start[:, at]), jnp.where(held, start[:, at], w[:, at])
            d_tile = d[:, at]
            for k in range(doubles - 1):
                same = colour_of(k) * colour_of(k + 1) > 0
                z, zc, d_tile = double_step((z, zc, d_tile), index_ref[k], sign_ref[k], same)
            t = jnp.where(colour_of(doubles - 1) > 0, zc, z)
            t, d_tile = last_step((z, t, d_tile), last_places, last_sign)
            turned.append(t)
            energies.append(d_tile)
        if tiles == 1:
            t, energy_ref[...] = turned[0], energies[0]
        else:
            energy_ref[...] = moved(jnp.concatenate(energies, axis=1), pair)
            t = moved(jnp.concatenate(turned, axis=1), pair)
        whole = jnp.concatenate([0.5 * t] * (cols // pair), axis=0)
        return jnp.where(square_row // pair == arrivals // pair, whole, 0.0)

    def one_round(round_index, carry):
        whole = sweep()
        half_way = dot_full(c_ref[...], whole)
        c_ref[...] = dot_full(whole, half_way, 0, 0)
        q_ref[...] = dot_full(q_ref[...], whole)
        return carry

    lax.fori_loop(0, ROUNDS - 1, one_round, 0)
    q_ref[...] = dot_full(q_ref[...], sweep())
    place = place_ref[0]
    to_front = lax.rem(cols - place * pair, cols)
    mean_ref[...] = pltpu.roll(energy_ref[...], to_front, 1)[0:1, 0:pair] / n_cells
    for d in range(cols // pair):
        rows = q_ref[pl.ds(pl.multiple_of((place ^ d) * pair, pair), pair), :]
        modes_ref[d * pair : (d + 1) * pair] = pltpu.roll(rows, to_front, 1)[:, 0:pair]


def in_vmem(n):
    return [pl.BlockSpec(memory_space=pltpu.VMEM)] * n


def tables_of(plan):
    n_steps, pair = plan.shape
    plan = jnp.concatenate([plan, jnp.arange(pair, dtype=jnp.int32)[None]], axis=0)
    shape = ((n_steps + 1) // 2, 8, LANES)
    return pl.pallas_call(
        table_kernel,
        out_shape=(jax.ShapeDtypeStruct(shape, jnp.int32), jax.ShapeDtypeStruct(shape, jnp.float32)),
        in_specs=in_vmem(1),
        out_specs=in_vmem(2),
        scratch_shapes=[pltpu.VMEM((n_steps + 1, LANES), jnp.int32)],
        name="step_tables",
    )(plan)


def turn_all(gram, tables, place, n_cells):
    cols = gram.shape[1]
    pair = 2 * tables[0].shape[0]
    return pl.pallas_call(
        functools.partial(turn_kernel, n_cells),
        out_shape=(
            jax.ShapeDtypeStruct((cols, pair), jnp.float32),
            jax.ShapeDtypeStruct((1, pair), jnp.float32),
        ),
        in_specs=in_vmem(3) + [pl.BlockSpec(memory_space=pltpu.SMEM)],
        out_specs=in_vmem(2),
        scratch_shapes=[
            pltpu.VMEM((8, cols), jnp.float32),
            pltpu.VMEM((cols, cols), jnp.float32),
            pltpu.VMEM((cols, cols), jnp.float32),
        ],
        compiler_params=pltpu.CompilerParams(vmem_limit_bytes=48 * 1024 * 1024),
        name="all_rounds",
    )(gram, *tables, place)


def sent(value, axis, toggle):
    return lax.ppermute(value, axis, [(i, i ^ toggle) for i in range(lax.axis_size(axis))])


def tree_sum(values):
    while len(values) > 1:
        values = [a + b for a, b in zip(values[::2], values[1::2])]
    return values[0]


def packed(gram):
    cols = gram.shape[0]
    half, three = cols // 2, cols // 4 * 3
    corner = jnp.concatenate([gram[three:, three:], jnp.zeros((cols - three, half - (cols - three)), gram.dtype)], axis=1)
    return jnp.concatenate([gram[:half], jnp.concatenate([corner, gram[half:three, half:]], axis=1)], axis=0)


def on_device(snapshots, plan):
    pair, cells = snapshots.shape
    n_blk, n_cell = lax.axis_size("blk"), lax.axis_size("cell")
    here = lax.axis_index("blk")
    place = here.astype(jnp.int32)[None]
    part = cells // n_blk

    def part_for(d):
        return lax.dynamic_slice_in_dim(snapshots, (here ^ d) * part, part, 1)

    parts = jnp.stack([part_for(0)] + [sent(part_for(d), "blk", d) for d in range(1, n_blk)])
    parts = [lax.dynamic_index_in_dim(parts, here ^ q, 0, keepdims=False) for q in range(n_blk)]
    tables, parts = lax.optimization_barrier((tables_of(plan), parts))
    whole = jnp.concatenate(parts, axis=0)
    gram = lax.dot_general(whole, whole, (((1,), (1,)), ((), ())), precision=lax.Precision.HIGHEST)
    gram = packed(gram)
    gram = gram + sent(gram, "cell", 1)
    gram = tree_sum([gram] + [sent(gram, "blk", d) for d in range(1, n_blk)])
    gram, held = lax.optimization_barrier((gram, snapshots))
    blocks = [snapshots] + [sent(held, "blk", d) for d in range(1, n_blk)]
    gram = tree_sum([gram] + [sent(gram, "cell", d) for d in range(2, n_cell, 2)])
    modes, energy = turn_all(gram, tables, place, cells * n_cell)
    rotated = lax.dot_general(
        modes, jnp.concatenate(blocks, axis=0), (((0,), (0,)), ((), ())), precision=lax.Precision.HIGH
    )
    return rotated * rotated, energy.reshape(pair)


def solution(mesh):
    return jax.shard_map(
        on_device,
        mesh=mesh,
        in_specs=(P("blk", "cell"), P()),
        out_specs=(P("blk", "cell"), P("blk")),
        check_vma=False,
    )
```

```python
import functools

import jax
import jax.numpy as jnp
from jax import lax
from jax.experimental import pallas as pl
from jax.experimental.pallas import tpu as pltpu
from jax.sharding import PartitionSpec as P

ROUNDS = 7
TINY_SQUARE = 2.0**-78
UP = 2.0**80
FLOOR = 2.0**-124
FLOOR_ROOT = 2.0**-62
LANES = 128


def split3(x):
    high = x.astype(jnp.bfloat16)
    rest = x - high.astype(jnp.float32)
    middle = rest.astype(jnp.bfloat16)
    low = (rest - middle.astype(jnp.float32)).astype(jnp.bfloat16)
    return high, middle, low


def dot_full(a, b, contract_a=1, contract_b=0):
    a0, a1, a2 = split3(a)
    b0, b1, b2 = split3(b)

    def one(x, y):
        return lax.dot_general(
            x, y, (((contract_a,), (contract_b,)), ((), ())), preferred_element_type=jnp.float32
        )

    small = one(a0, b2) + one(a2, b0) + one(a1, b1)
    return one(a0, b0) + ((one(a0, b1) + one(a1, b0)) + small)


def turning(twice_cross, own, other, sign, square_stretch=None, shrink=None):
    spread = (own - other) * sign
    up_cross, up_spread = twice_cross * UP, spread * UP
    if shrink is None:
        spread_square, up_spread_square = spread * spread, up_spread * up_spread + FLOOR
    else:
        spread_square = (spread * spread) * square_stretch
        up_spread_square = (up_spread * up_spread) * square_stretch + FLOOR
    square = spread_square + twice_cross * twice_cross
    up_square = up_spread_square + up_cross * up_cross
    is_small = square < TINY_SQUARE
    norm_square = jnp.where(is_small, up_square, square)
    size = jnp.abs(jnp.where(is_small, up_spread, spread))
    half_norm = norm_square * jnp.where(is_small, (0.5 / UP) * sign, 0.5 * sign)
    if shrink is not None:
        size = size * (square_stretch * shrink)
        half_norm = half_norm * shrink
    size = jnp.maximum(size, FLOOR_ROOT)
    cross = jnp.where(is_small, up_cross, twice_cross) * sign
    cross_sign = jnp.where(twice_cross < 0, -sign, sign)
    in_order = spread >= 0
    inverse = lax.rsqrt(norm_square)
    large = size * inverse + 1.0
    square_uv = (size + size) * inverse + 2.0
    small = cross * inverse
    u = jnp.where(in_order, large, jnp.abs(small))
    v = jnp.where(in_order, small, cross_sign * large)
    return u, v, lax.rsqrt(square_uv), 0.5 * (own + other) + half_norm * inverse, square_uv


def gather(x, index):
    return jnp.take_along_axis(x, jnp.broadcast_to(index, x.shape), axis=1)


def tall(x, like):
    return jnp.concatenate([x] * (like.shape[0] // x.shape[0]), axis=0)


def turned_by(c, s, x, y):
    return tall(c, x) * x + tall(s, x) * y


def product(x, y):
    return jnp.sum(x * y, axis=0, keepdims=True)


def last_step(state, places, sign):
    z, t, d, g = state
    (zi, ti, di, gi), (zp, tp, dp, gp) = [[gather(x, place) for x in state] for place in places]
    u, v, f, d, _ = turning((gi * gp) * product(zi, zp), di, dp, sign)
    return turned_by(u * f * gi, v * f * gp, ti, tp), d


def double_step(state, index_tile, sign_tile, same):
    z, zc, d, g = state
    p, q, pq = [index_tile[k : k + 1] for k in range(3)]
    sign, sign_q, sign_next = [sign_tile[k : k + 1] for k in range(3)]
    zp, zq, zpq = gather(z, p), gather(z, q), gather(z, pq)
    rows = lax.broadcasted_iota(jnp.int32, d.shape, 0)
    both = jnp.take_along_axis(jnp.where(rows < 4, d, g), index_tile, axis=1)
    dp, dq, dpq, _, gp, gq, gpq = [jnp.broadcast_to(both[k : k + 1], d.shape) for k in range(7)]
    zcq, zcp, zcpq = gather(zc, q), gather(zc, p), gather(zc, pq)
    u, v, f, d1, n = turning((g * gp) * product(z, zp), d, dp, sign)
    uq, vq, fq, d1q, nq = turning((gq * gpq) * product(zq, zpq), dq, dpq, sign_q)
    e00, e11 = (g * gq) * product(z, zq), (gp * gpq) * product(zp, zpq)
    e01, e10 = (g * gpq) * product(zc, zpq), (gp * gq) * product(zp, zcq)
    cross = ((u * uq) * e00 + (v * vq) * e11) + ((u * vq) * e01 + (v * uq) * e10)
    u1, v1, f1, d2, _ = turning(cross, d1, d1q, sign_next, n * nq, f * fq)
    c, s, cq, sq = u * (f * g), v * (f * gp), uq * (fq * gq), vq * (fq * gpq)
    z1, zc1 = turned_by(c, s, z, zcp), turned_by(c, s, zc, zp)
    zq1, zcq1 = turned_by(cq, sq, zq, zcpq), turned_by(cq, sq, zcq, zpq)
    own, other = jnp.where(same, z1, zc1), jnp.where(same, zcq1, zq1)
    own_c, other_c = jnp.where(same, zc1, z1), jnp.where(same, zq1, zcq1)
    return turned_by(u1, v1, own, other), turned_by(u1, v1, own_c, other_c), d2, f1


def moved(x, pair):
    cols, half = x.shape[1], pair // 2
    place = lax.broadcasted_iota(jnp.int32, x.shape, 1)
    is_upper = place % pair < half
    from_own = (place < half) & is_upper
    shifted = ((place // pair == 1) & is_upper) | (place >= cols - half)
    right, left, by_half = pltpu.roll(x, pair, 1), pltpu.roll(x, cols - pair, 1), pltpu.roll(x, half, 1)
    return jnp.where(from_own, x, jnp.where(shifted, by_half, jnp.where(is_upper, right, left)))


def unpacked(x):
    cols = x.shape[1]
    half, quarter = cols // 2, cols // 4
    low = x[half:]
    upper = jnp.concatenate([x[:half], low, pltpu.roll(low, 3 * quarter, 1)], axis=0)
    row = lax.broadcasted_iota(jnp.int32, (cols, cols), 0) // quarter
    lane = lax.broadcasted_iota(jnp.int32, (cols, cols), 1) // quarter
    return jnp.where(lane >= row, upper, upper.T)


def sign_of(own, other):
    return jnp.where(own < other, 1.0, -1.0).astype(jnp.float32)


def table_kernel(plan_ref, index_ref, sign_ref, table_ref):
    pair = plan_ref.shape[1]
    doubles = pair // 2
    table = plan_ref[...]
    table_ref[...] = jnp.concatenate([table + pair * g for g in range(LANES // pair)], axis=1)
    first = table_ref[pl.ds(0, doubles, stride=2), :]
    second = table_ref[pl.ds(1, doubles, stride=2), :]
    own = lax.broadcasted_iota(jnp.int32, (doubles, LANES), 1)
    first_of_second = jnp.take_along_axis(first, second, axis=1)
    around = jnp.take_along_axis(second, first, axis=1)
    least = own
    reach = 1
    while reach < doubles:
        least = jnp.minimum(least, jnp.take_along_axis(least, around, axis=1))
        around = jnp.take_along_axis(around, around, axis=1)
        reach *= 2
    colour = sign_of(least, jnp.take_along_axis(least, first, axis=1))
    lower = sign_of(own, first)
    is_last = lax.broadcasted_iota(jnp.int32, (doubles, LANES), 0) == doubles - 1
    colour = jnp.where(is_last, lower, colour)
    signs = [lower, sign_of(second, first_of_second), sign_of(own, second), colour]
    for k in range(doubles):
        at = slice(k, k + 1)
        index_ref[k] = jnp.concatenate([first[at], second[at], first_of_second[at], own[at]] * 2, axis=0)
        sign_ref[k] = jnp.concatenate([x[at] for x in signs] + [lower[at]] * 4, axis=0)


def turn_kernel(n_cells, gram_ref, index_ref, sign_ref, place_ref, modes_ref, mean_ref, energy_ref, c_ref, q_ref):
    cols = gram_ref.shape[1]
    doubles = index_ref.shape[0]
    pair = 2 * doubles
    tiles = cols // LANES
    square_row = lax.broadcasted_iota(jnp.int32, (cols, cols), 0)
    square_lane = lax.broadcasted_iota(jnp.int32, (cols, cols), 1)
    own_pair = square_row // pair == square_lane // pair
    is_diag = (square_row == square_lane % pair)[0:pair]
    start = jnp.where(is_diag, 2.0, 0.0)
    c_ref[...] = unpacked(gram_ref[...])
    q_ref[...] = (square_row == square_lane).astype(jnp.float32)

    arrivals = moved(lax.broadcasted_iota(jnp.int32, (8, cols), 1), pair)
    last = jnp.broadcast_to(index_ref[doubles - 1][0:1], (8, LANES))
    if tiles == 1:
        last_places = [arrivals, gather(last, arrivals)]
    else:
        last_places = [lax.broadcasted_iota(jnp.int32, (8, LANES), 1), last]
    last_places = [x[0:1] for x in last_places]
    last_sign = sign_of(*last_places)
    arrivals = arrivals[0:1]

    def colour_of(k):
        return sign_ref[k][3:4]

    def sweep():
        kept = jnp.where(own_pair, c_ref[...], 0.0)
        w = kept[0:pair]
        for p in range(1, cols // pair):
            w = w + kept[p * pair : (p + 1) * pair]
        d = jnp.broadcast_to(jnp.sum(jnp.where(is_diag, w, 0.0), axis=0, keepdims=True), (8, cols))
        turned, energies = [], []
        for tile in range(tiles):
            at = slice(tile * LANES, (tile + 1) * LANES)
            held = colour_of(0) > 0
            z, zc = jnp.where(held, w[:, at], start[:, at]), jnp.where(held, start[:, at], w[:, at])
            d_tile, g = d[:, at], jnp.ones((8, LANES), jnp.float32)
            for k in range(doubles - 1):
                same = colour_of(k) * colour_of(k + 1) > 0
                z, zc, d_tile, g = double_step((z, zc, d_tile, g), index_ref[k], sign_ref[k], same)
            t = jnp.where(colour_of(doubles - 1) > 0, zc, z)
            t, d_tile = last_step((z, t, d_tile, g), last_places, last_sign)
            turned.append(t)
            energies.append(d_tile)
        if tiles == 1:
            t, energy_ref[...] = turned[0], energies[0]
        else:
            energy_ref[...] = moved(jnp.concatenate(energies, axis=1), pair)
            t = moved(jnp.concatenate(turned, axis=1), pair)
        whole = jnp.concatenate([0.5 * t] * (cols // pair), axis=0)
        return jnp.where(square_row // pair == arrivals // pair, whole, 0.0)

    def one_round(round_index, carry):
        whole = sweep()
        half_way = dot_full(c_ref[...], whole)
        c_ref[...] = dot_full(whole, half_way, 0, 0)
        q_ref[...] = dot_full(q_ref[...], whole)
        return carry

    lax.fori_loop(0, ROUNDS - 1, one_round, 0)
    q_ref[...] = dot_full(q_ref[...], sweep())
    place = place_ref[0]
    to_front = lax.rem(cols - place * pair, cols)
    mean_ref[...] = pltpu.roll(energy_ref[...], to_front, 1)[0:1, 0:pair] / n_cells
    for d in range(cols // pair):
        rows = q_ref[pl.ds(pl.multiple_of((place ^ d) * pair, pair), pair), :]
        modes_ref[d * pair : (d + 1) * pair] = pltpu.roll(rows, to_front, 1)[:, 0:pair]


def in_vmem(n):
    return [pl.BlockSpec(memory_space=pltpu.VMEM)] * n


def tables_of(plan):
    n_steps, pair = plan.shape
    plan = jnp.concatenate([plan, jnp.arange(pair, dtype=jnp.int32)[None]], axis=0)
    shape = ((n_steps + 1) // 2, 8, LANES)
    return pl.pallas_call(
        table_kernel,
        out_shape=(jax.ShapeDtypeStruct(shape, jnp.int32), jax.ShapeDtypeStruct(shape, jnp.float32)),
        in_specs=in_vmem(1),
        out_specs=in_vmem(2),
        scratch_shapes=[pltpu.VMEM((n_steps + 1, LANES), jnp.int32)],
        name="step_tables",
    )(plan)


def turn_all(gram, tables, place, n_cells):
    cols = gram.shape[1]
    pair = 2 * tables[0].shape[0]
    return pl.pallas_call(
        functools.partial(turn_kernel, n_cells),
        out_shape=(
            jax.ShapeDtypeStruct((cols, pair), jnp.float32),
            jax.ShapeDtypeStruct((1, pair), jnp.float32),
        ),
        in_specs=in_vmem(3) + [pl.BlockSpec(memory_space=pltpu.SMEM)],
        out_specs=in_vmem(2),
        scratch_shapes=[
            pltpu.VMEM((8, cols), jnp.float32),
            pltpu.VMEM((cols, cols), jnp.float32),
            pltpu.VMEM((cols, cols), jnp.float32),
        ],
        compiler_params=pltpu.CompilerParams(vmem_limit_bytes=48 * 1024 * 1024),
        name="all_rounds",
    )(gram, *tables, place)


def sent(value, axis, toggle):
    return lax.ppermute(value, axis, [(i, i ^ toggle) for i in range(lax.axis_size(axis))])


def tree_sum(values):
    while len(values) > 1:
        values = [a + b for a, b in zip(values[::2], values[1::2])]
    return values[0]


def packed(gram):
    cols = gram.shape[0]
    half, three = cols // 2, cols // 4 * 3
    corner = jnp.concatenate([gram[three:, three:], jnp.zeros((cols - three, half - (cols - three)), gram.dtype)], axis=1)
    return jnp.concatenate([gram[:half], jnp.concatenate([corner, gram[half:three, half:]], axis=1)], axis=0)


def on_device(snapshots, plan):
    pair, cells = snapshots.shape
    n_blk, n_cell = lax.axis_size("blk"), lax.axis_size("cell")
    here = lax.axis_index("blk")
    place = here.astype(jnp.int32)[None]
    part = cells // n_blk

    def part_for(d):
        return lax.dynamic_slice_in_dim(snapshots, (here ^ d) * part, part, 1)

    parts = jnp.stack([part_for(0)] + [sent(part_for(d), "blk", d) for d in range(1, n_blk)])
    parts = [lax.dynamic_index_in_dim(parts, here ^ q, 0, keepdims=False) for q in range(n_blk)]
    tables, parts = lax.optimization_barrier((tables_of(plan), parts))
    whole = jnp.concatenate(parts, axis=0)
    gram = lax.dot_general(whole, whole, (((1,), (1,)), ((), ())), precision=lax.Precision.HIGHEST)
    gram = packed(gram)
    gram = gram + sent(gram, "cell", 1)
    gram = tree_sum([gram] + [sent(gram, "blk", d) for d in range(1, n_blk)])
    gram, held = lax.optimization_barrier((gram, snapshots))
    blocks = [snapshots] + [sent(held, "blk", d) for d in range(1, n_blk)]
    gram = tree_sum([gram] + [sent(gram, "cell", d) for d in range(2, n_cell, 2)])
    modes, energy = turn_all(gram, tables, place, cells * n_cell)
    rotated = lax.dot_general(
        modes, jnp.concatenate(blocks, axis=0), (((0,), (0,)), ((), ())), precision=lax.Precision.HIGH
    )
    return rotated * rotated, energy.reshape(pair)


def solution(mesh):
    return jax.shard_map(
        on_device,
        mesh=mesh,
        in_specs=(P("blk", "cell"), P()),
        out_specs=(P("blk", "cell"), P("blk")),
        check_vma=False,
    )
```

```python
import functools

import jax
import jax.numpy as jnp
from jax import lax
from jax.experimental import pallas as pl
from jax.experimental.pallas import tpu as pltpu
from jax.sharding import PartitionSpec as P

ROUNDS = 7
TINY_SQUARE = 2.0**-78
UP = 2.0**80
FLOOR = 2.0**-124
FLOOR_ROOT = 2.0**-62
LANES = 128


def split3(x):
    high = x.astype(jnp.bfloat16)
    rest = x - high.astype(jnp.float32)
    middle = rest.astype(jnp.bfloat16)
    low = (rest - middle.astype(jnp.float32)).astype(jnp.bfloat16)
    return high, middle, low


def dot_full(a, b, contract_a=1, contract_b=0):
    a0, a1, a2 = split3(a)
    b0, b1, b2 = split3(b)

    def one(x, y):
        return lax.dot_general(
            x, y, (((contract_a,), (contract_b,)), ((), ())), preferred_element_type=jnp.float32
        )

    small = one(a0, b2) + one(a2, b0) + one(a1, b1)
    return one(a0, b0) + ((one(a0, b1) + one(a1, b0)) + small)


def turning(twice_cross, own, other, sign, square_stretch=None, shrink=None):
    spread = (own - other) * sign
    up_cross, up_spread = twice_cross * UP, spread * UP
    if shrink is None:
        spread_square, up_spread_square = spread * spread, up_spread * up_spread + FLOOR
    else:
        spread_square = (spread * spread) * square_stretch
        up_spread_square = (up_spread * up_spread) * square_stretch + FLOOR
    square = spread_square + twice_cross * twice_cross
    up_square = up_spread_square + up_cross * up_cross
    is_small = square < TINY_SQUARE
    norm_square = jnp.where(is_small, up_square, square)
    size = jnp.abs(jnp.where(is_small, up_spread, spread))
    half_norm = norm_square * jnp.where(is_small, (0.5 / UP) * sign, 0.5 * sign)
    if shrink is not None:
        size = size * (square_stretch * shrink)
        half_norm = half_norm * shrink
    size = jnp.maximum(size, FLOOR_ROOT)
    cross = jnp.where(is_small, up_cross, twice_cross) * sign
    cross_sign = jnp.where(twice_cross < 0, -sign, sign)
    in_order = spread >= 0
    inverse = lax.rsqrt(norm_square)
    large = size * inverse + 1.0
    square_uv = (size + size) * inverse + 2.0
    small = cross * inverse
    u = jnp.where(in_order, large, jnp.abs(small))
    v = jnp.where(in_order, small, cross_sign * large)
    return u, v, lax.rsqrt(square_uv), 0.5 * (own + other) + half_norm * inverse, square_uv


def gather(x, index):
    return jnp.take_along_axis(x, jnp.broadcast_to(index, x.shape), axis=1)


def tall(x, like):
    return jnp.concatenate([x] * (like.shape[0] // x.shape[0]), axis=0)


def turned_by(c, s, x, y):
    return tall(c, x) * x + tall(s, x) * y


def product(x, y):
    return jnp.sum(x * y, axis=0, keepdims=True)


def last_step(state, places, sign):
    z, t, d, g = state
    (zi, ti, di, gi), (zp, tp, dp, gp) = [[gather(x, place) for x in state] for place in places]
    u, v, f, d, _ = turning((gi * gp) * product(zi, zp), di, dp, sign)
    return turned_by(u * f * gi, v * f * gp, ti, tp), d


def double_step(state, index_tile, sign_tile, same):
    z, zc, d, g = state
    p, q, pq = [index_tile[k : k + 1] for k in range(3)]
    sign, sign_q, sign_next = [sign_tile[k : k + 1] for k in range(3)]
    zp, zq, zpq = gather(z, p), gather(z, q), gather(z, pq)
    rows = lax.broadcasted_iota(jnp.int32, d.shape, 0)
    both = jnp.take_along_axis(jnp.where(rows < 4, d, g), index_tile, axis=1)
    dp, dq, dpq, _, gp, gq, gpq = [jnp.broadcast_to(both[k : k + 1], d.shape) for k in range(7)]
    zcq, zcp, zcpq = gather(zc, q), gather(zc, p), gather(zc, pq)
    u, v, f, d1, n = turning((g * gp) * product(z, zp), d, dp, sign)
    uq, vq, fq, d1q, nq = turning((gq * gpq) * product(zq, zpq), dq, dpq, sign_q)
    e00, e11 = (g * gq) * product(z, zq), (gp * gpq) * product(zp, zpq)
    e01, e10 = (g * gpq) * product(zc, zpq), (gp * gq) * product(zp, zcq)
    cross = ((u * uq) * e00 + (v * vq) * e11) + ((u * vq) * e01 + (v * uq) * e10)
    u1, v1, f1, d2, _ = turning(cross, d1, d1q, sign_next, n * nq, f * fq)
    c, s, cq, sq = u * (f * g), v * (f * gp), uq * (fq * gq), vq * (fq * gpq)
    z1, zc1 = turned_by(c, s, z, zcp), turned_by(c, s, zc, zp)
    zq1, zcq1 = turned_by(cq, sq, zq, zcpq), turned_by(cq, sq, zcq, zpq)
    own, other = jnp.where(same, z1, zc1), jnp.where(same, zcq1, zq1)
    own_c, other_c = jnp.where(same, zc1, z1), jnp.where(same, zq1, zcq1)
    return turned_by(u1, v1, own, other), turned_by(u1, v1, own_c, other_c), d2, f1


def moved(x, pair):
    cols, half = x.shape[1], pair // 2
    place = lax.broadcasted_iota(jnp.int32, x.shape, 1)
    is_upper = place % pair < half
    from_own = (place < half) & is_upper
    shifted = ((place // pair == 1) & is_upper) | (place >= cols - half)
    right, left, by_half = pltpu.roll(x, pair, 1), pltpu.roll(x, cols - pair, 1), pltpu.roll(x, half, 1)
    return jnp.where(from_own, x, jnp.where(shifted, by_half, jnp.where(is_upper, right, left)))


def unpacked(x):
    cols = x.shape[1]
    half, quarter = cols // 2, cols // 4
    low = x[half:]
    upper = jnp.concatenate([x[:half], low, pltpu.roll(low, 3 * quarter, 1)], axis=0)
    row = lax.broadcasted_iota(jnp.int32, (cols, cols), 0) // quarter
    lane = lax.broadcasted_iota(jnp.int32, (cols, cols), 1) // quarter
    return jnp.where(lane >= row, upper, upper.T)


def sign_of(own, other):
    return jnp.where(own < other, 1.0, -1.0).astype(jnp.float32)


def table_kernel(plan_ref, index_ref, sign_ref, table_ref):
    pair = plan_ref.shape[1]
    doubles = pair // 2
    table = plan_ref[...]
    table_ref[...] = jnp.concatenate([table + pair * g for g in range(LANES // pair)], axis=1)
    first = table_ref[pl.ds(0, doubles, stride=2), :]
    second = table_ref[pl.ds(1, doubles, stride=2), :]
    own = lax.broadcasted_iota(jnp.int32, (doubles, LANES), 1)
    first_of_second = jnp.take_along_axis(first, second, axis=1)
    around = jnp.take_along_axis(second, first, axis=1)
    least = own
    reach = 1
    while reach < doubles:
        least = jnp.minimum(least, jnp.take_along_axis(least, around, axis=1))
        around = jnp.take_along_axis(around, around, axis=1)
        reach *= 2
    colour = sign_of(least, jnp.take_along_axis(least, first, axis=1))
    lower = sign_of(own, first)
    is_last = lax.broadcasted_iota(jnp.int32, (doubles, LANES), 0) == doubles - 1
    colour = jnp.where(is_last, lower, colour)
    signs = [lower, sign_of(second, first_of_second), sign_of(own, second), colour]
    for k in range(doubles):
        at = slice(k, k + 1)
        index_ref[k] = jnp.concatenate([first[at], second[at], first_of_second[at], own[at]] * 2, axis=0)
        sign_ref[k] = jnp.concatenate([x[at] for x in signs] + [lower[at]] * 4, axis=0)


def turn_kernel(n_cells, gram_ref, index_ref, sign_ref, place_ref, modes_ref, mean_ref, energy_ref, c_ref, q_ref):
    cols = gram_ref.shape[1]
    doubles = index_ref.shape[0]
    pair = 2 * doubles
    tiles = cols // LANES
    square_row = lax.broadcasted_iota(jnp.int32, (cols, cols), 0)
    square_lane = lax.broadcasted_iota(jnp.int32, (cols, cols), 1)
    own_pair = square_row // pair == square_lane // pair
    is_diag = (square_row == square_lane % pair)[0:pair]
    start = jnp.where(is_diag, 2.0, 0.0)
    c_ref[...] = unpacked(gram_ref[...])
    q_ref[...] = (square_row == square_lane).astype(jnp.float32)

    arrivals = moved(lax.broadcasted_iota(jnp.int32, (8, cols), 1), pair)
    last = jnp.broadcast_to(index_ref[doubles - 1][0:1], (8, LANES))
    if tiles == 1:
        last_places = [arrivals, gather(last, arrivals)]
    else:
        last_places = [lax.broadcasted_iota(jnp.int32, (8, LANES), 1), last]
    last_places = [x[0:1] for x in last_places]
    last_sign = sign_of(*last_places)
    arrivals = arrivals[0:1]

    def colour_of(k):
        return sign_ref[k][3:4]

    def sweep():
        kept = jnp.where(own_pair, c_ref[...], 0.0)
        w = kept[0:pair]
        for p in range(1, cols // pair):
            w = w + kept[p * pair : (p + 1) * pair]
        d = jnp.broadcast_to(jnp.sum(jnp.where(is_diag, w, 0.0), axis=0, keepdims=True), (8, cols))
        turned, energies = [], []
        for tile in range(tiles):
            at = slice(tile * LANES, (tile + 1) * LANES)
            held = colour_of(0) > 0
            z, zc = jnp.where(held, w[:, at], start[:, at]), jnp.where(held, start[:, at], w[:, at])
            d_tile, g = d[:, at], jnp.ones((8, LANES), jnp.float32)
            for k in range(doubles - 1):
                same = colour_of(k) * colour_of(k + 1) > 0
                z, zc, d_tile, g = double_step((z, zc, d_tile, g), index_ref[k], sign_ref[k], same)
            t = jnp.where(colour_of(doubles - 1) > 0, zc, z)
            t, d_tile = last_step((z, t, d_tile, g), last_places, last_sign)
            turned.append(t)
            energies.append(d_tile)
        if tiles == 1:
            t, energy_ref[...] = turned[0], energies[0]
        else:
            energy_ref[...] = moved(jnp.concatenate(energies, axis=1), pair)
            t = moved(jnp.concatenate(turned, axis=1), pair)
        whole = jnp.concatenate([0.5 * t] * (cols // pair), axis=0)
        return jnp.where(square_row // pair == arrivals // pair, whole, 0.0)

    def one_round(round_index, carry):
        whole = sweep()
        half_way = dot_full(c_ref[...], whole)
        c_ref[...] = dot_full(whole, half_way, 0, 0)
        q_ref[...] = dot_full(q_ref[...], whole)
        return carry

    lax.fori_loop(0, ROUNDS - 1, one_round, 0)
    q_ref[...] = dot_full(q_ref[...], sweep())
    place = place_ref[0]
    to_front = lax.rem(cols - place * pair, cols)
    mean_ref[...] = pltpu.roll(energy_ref[...], to_front, 1)[0:1, 0:pair] / n_cells
    for d in range(cols // pair):
        rows = q_ref[pl.ds(pl.multiple_of((place ^ d) * pair, pair), pair), :]
        modes_ref[d * pair : (d + 1) * pair] = pltpu.roll(rows, to_front, 1)[:, 0:pair]


def in_vmem(n):
    return [pl.BlockSpec(memory_space=pltpu.VMEM)] * n


def tables_of(plan):
    n_steps, pair = plan.shape
    plan = jnp.concatenate([plan, jnp.arange(pair, dtype=jnp.int32)[None]], axis=0)
    shape = ((n_steps + 1) // 2, 8, LANES)
    return pl.pallas_call(
        table_kernel,
        out_shape=(jax.ShapeDtypeStruct(shape, jnp.int32), jax.ShapeDtypeStruct(shape, jnp.float32)),
        in_specs=in_vmem(1),
        out_specs=in_vmem(2),
        scratch_shapes=[pltpu.VMEM((n_steps + 1, LANES), jnp.int32)],
        name="step_tables",
    )(plan)


def turn_all(gram, tables, place, n_cells):
    cols = gram.shape[1]
    pair = 2 * tables[0].shape[0]
    return pl.pallas_call(
        functools.partial(turn_kernel, n_cells),
        out_shape=(
            jax.ShapeDtypeStruct((cols, pair), jnp.float32),
            jax.ShapeDtypeStruct((1, pair), jnp.float32),
        ),
        in_specs=in_vmem(3) + [pl.BlockSpec(memory_space=pltpu.SMEM)],
        out_specs=in_vmem(2),
        scratch_shapes=[
            pltpu.VMEM((8, cols), jnp.float32),
            pltpu.VMEM((cols, cols), jnp.float32),
            pltpu.VMEM((cols, cols), jnp.float32),
        ],
        compiler_params=pltpu.CompilerParams(vmem_limit_bytes=48 * 1024 * 1024),
        name="all_rounds",
    )(gram, *tables, place)


def sent(value, axis, toggle):
    return lax.ppermute(value, axis, [(i, i ^ toggle) for i in range(lax.axis_size(axis))])


def tree_sum(values):
    while len(values) > 1:
        values = [a + b for a, b in zip(values[::2], values[1::2])]
    return values[0]


def packed(gram):
    cols = gram.shape[0]
    half, three = cols // 2, cols // 4 * 3
    corner = jnp.concatenate([gram[three:, three:], jnp.zeros((cols - three, half - (cols - three)), gram.dtype)], axis=1)
    return jnp.concatenate([gram[:half], jnp.concatenate([corner, gram[half:three, half:]], axis=1)], axis=0)


def on_device(snapshots, plan):
    pair, cells = snapshots.shape
    n_blk, n_cell = lax.axis_size("blk"), lax.axis_size("cell")
    here = lax.axis_index("blk")
    place = here.astype(jnp.int32)[None]
    part = cells // n_blk

    def run_of(x, first, count):
        twice = jnp.concatenate([x, x], axis=1)
        return lax.dynamic_slice_in_dim(twice, lax.rem(first, n_blk) * part, count * part, 1)

    def part_for(d):
        return lax.dynamic_slice_in_dim(snapshots, (here ^ d) * part, part, 1)

    arrived = [part_for(0)] + [sent(part_for(d), "blk", d) for d in range(1, n_blk)]
    tables, source = lax.optimization_barrier((tables_of(plan), snapshots))
    rest = [run_of(source, (here ^ d) + 1, n_blk - 1) for d in range(1, n_blk)]
    own = run_of(source, here, n_blk)
    parts = jnp.stack(arrived)
    parts = [lax.dynamic_index_in_dim(parts, here ^ q, 0, keepdims=False) for q in range(n_blk)]
    tables, rest, own, parts = lax.optimization_barrier((tables, rest, own, parts))
    whole = jnp.concatenate(parts, axis=0)
    gram = lax.dot_general(whole, whole, (((1,), (1,)), ((), ())), precision=lax.Precision.HIGHEST)
    gram = packed(gram)
    gram = gram + sent(gram, "cell", 1)
    gram, rest = lax.optimization_barrier((gram, rest))
    others = [sent(rest[0], "blk", 1)]
    gram = tree_sum([gram] + [sent(gram, "blk", d) for d in range(1, n_blk)])
    gram, rest = lax.optimization_barrier((gram, rest))
    others += [sent(rest[d - 1], "blk", d) for d in range(len(others) + 1, n_blk)]
    blocks = [own] + [jnp.concatenate(x, axis=1) for x in zip(arrived[1:], others)]
    gram = tree_sum([gram] + [sent(gram, "cell", d) for d in range(2, n_cell, 2)])
    modes, energy = turn_all(gram, tables, place, cells * n_cell)
    rotated = lax.dot_general(
        modes, jnp.concatenate(blocks, axis=0), (((0,), (0,)), ((), ())), precision=lax.Precision.HIGH
    )
    return run_of(rotated * rotated, n_blk - here, n_blk), energy.reshape(pair)


def solution(mesh):
    return jax.shard_map(
        on_device,
        mesh=mesh,
        in_specs=(P("blk", "cell"), P()),
        out_specs=(P("blk", "cell"), P("blk")),
        check_vma=False,
    )
```
